32 devices in a mesh: groups: 2 (over x), hid: 16 (over z, y, core).
Axes of the slice: x: 2, y: 2, z: 4, core: 2. Of those that a mesh axis runs over, the one named last changes fastest.
Arguments:
- tokens: bfloat16 [512, 6144], P('groups', 'hid'), parts along dimension 0, may hold values from -6 to 6
- upstream: bfloat16 [512, 6144], P('groups', 'hid'), parts along dimension 0, may hold values from -6 to 6
- loss_mask: int32 [512], P('groups'), parts along dimension 0, may hold values from 0 to 1, as said below
- gate_weight: bfloat16 [6144, 23552], P(None, 'hid'), may hold values from -0.109375 to 0.109375
- up_weight: bfloat16 [6144, 23552], P(None, 'hid'), may hold values from -0.109375 to 0.109375
- down_weight: bfloat16 [23552, 6144], P('hid'), may hold values from -0.0546875 to 0.0546875
Outputs:
- ffn_output: bfloat16 [512, 6144], P('groups', 'hid'), parts along dimension 0
- token_grad: bfloat16 [512, 6144], P('groups', 'hid'), parts along dimension 0
- gate_grad: bfloat16 [12288, 23552], P('groups', 'hid'), parts along dimension 0
- up_grad: bfloat16 [12288, 23552], P('groups', 'hid'), parts along dimension 0
- down_grad: bfloat16 [23552, 12288], P('hid', 'groups'), parts along dimension 1
The draws below stay inside these ranges and needn't reach their ends.
There are 2 independent parts, one for each index of `groups`. The reference program is written for one: setup_inputs(seed, part) draws one part's arguments, and reference() takes and returns one part's arrays. A program takes and returns all parts, laid end to end along the dimension named above; an argument that names none is the same for every part. Nothing has to cross between parts.
Inputs may be any that keep to these rules, and one draw needn't show every extreme that they name: `loss_mask`: exactly 128 of the 256 tokens have mask 1.
All inputs are finite; a program needn't handle non-finite values.
Results may differ from the reference program's by a relative error of at most 0.005.
Values may be sent and summed in bfloat16 or wider, within the bound.
No kernel may reach another device: no remote copies, remote signals or barrier semaphores. Data moves between devices by JAX's collectives and lax.ppermute only.
A program may use at most 256 MiB of HBM per device.

```python
import jax
import jax.numpy as jnp

D = 6144
FF = 23552
TOK = 256
LIVE = 128


def draw_loss_mask(key, part):
    key = jax.random.fold_in(key, 7)
    order = jax.random.permutation(key, TOK)
    return (order < LIVE).astype(jnp.int32)


def raised(entries, own_key, source, target, shards_of, factor):
    def block_of(position):
        return (jnp.arange(entries.shape[position]) // (entries.shape[position] // shards_of)).reshape((-1,) + (1,) * (entries.ndim - 1 - position))

    near = jax.random.permutation(own_key, shards_of)[block_of(target)]
    second = (block_of(target) + shards_of // 2) % shards_of
    return jnp.where((block_of(source) == near) | (block_of(source) == second), factor * entries, entries)


def level_of(rng, dims, cuts, low, top_value):
    def one(dim, shards_of):
        heights = jax.random.uniform(jax.random.fold_in(jax.random.fold_in(rng, 6), dim), (shards_of,), jnp.float32, low / len(cuts), top_value / len(cuts))
        return jnp.repeat(jnp.exp(heights), dims[dim] // shards_of).reshape((-1,) + (1,) * (len(dims) - dim - 1))

    factor_of = one(*cuts[0])
    for cut in cuts[1:]:
        factor_of = factor_of * one(*cut)
    return factor_of


def gaussian(rng, dims, spread, reach, cuts=(), kind=jnp.bfloat16):
    values = spread * jax.random.normal(rng, dims, jnp.float32)
    if cuts:
        values = values * level_of(rng, dims, cuts, -0.22, 0.18)
    return jnp.clip(values, -reach, reach).astype(kind)


def gaussian_with(stream_key, shape, scale, bound, cuts, heavy, held_as=jnp.bfloat16):
    result = scale * jax.random.normal(stream_key, shape, jnp.float32)
    if cuts:
        result = result * level_of(stream_key, shape, cuts, -0.22, 0.18)
    return jnp.clip(raised(result, jax.random.fold_in(stream_key, 3), *heavy), -bound, bound).astype(held_as)


def setup_inputs(seed: int = 0, part: int = 0) -> dict:
    key_of = jax.random.split(jax.random.key(seed), 7)
    part_splits = jax.random.split(jax.random.fold_in(key_of[6], part), 7)
    return {
        "tokens": gaussian(part_splits[0], (TOK, D), 1.0, 6.0, ((1, 16),)),
        "upstream": gaussian(part_splits[1], (TOK, D), 1.0, 6.0, ((1, 16),)),
        "loss_mask": draw_loss_mask(jax.random.fold_in(jax.random.fold_in(key_of[6], part), 71), part),
        "gate_weight": gaussian_with(key_of[3], (D, FF), D ** -0.5, 0.109375, ((1, 16),), (1, 0, 16, 2.0)),
        "up_weight": gaussian_with(key_of[4], (D, FF), D ** -0.5, 0.109375, ((1, 16),), (1, 0, 16, 2.0)),
        "down_weight": gaussian_with(key_of[5], (FF, D), FF ** -0.5, 0.0546875, ((0, 16),), (0, 1, 16, 2.0)),
    }


def reference(tokens, upstream, loss_mask, gate_weight, up_weight, down_weight):
    gate_lin = jnp.dot(tokens, gate_weight, preferred_element_type=jnp.float32)
    up_lin = jnp.dot(tokens, up_weight, preferred_element_type=jnp.float32)
    sigmoid_gate = jax.nn.sigmoid(gate_lin)
    activated = gate_lin * sigmoid_gate
    hidden = (activated * up_lin).astype(jnp.bfloat16)
    ffn_output = jnp.dot(hidden, down_weight, preferred_element_type=jnp.float32).astype(jnp.bfloat16)
    masked = upstream * loss_mask[:, None].astype(upstream.dtype)
    d_hidden = jnp.dot(masked, down_weight.T, preferred_element_type=jnp.float32)
    d_up = (d_hidden * activated).astype(jnp.bfloat16)
    d_gate = (d_hidden * up_lin * sigmoid_gate * (1.0 + gate_lin * (1.0 - sigmoid_gate))).astype(jnp.bfloat16)
    down_grad = jnp.dot(hidden.T, masked, preferred_element_type=jnp.float32).astype(jnp.bfloat16)
    gate_grad = jnp.dot(tokens.T, d_gate, preferred_element_type=jnp.float32).astype(jnp.bfloat16)
    up_grad = jnp.dot(tokens.T, d_up, preferred_element_type=jnp.float32).astype(jnp.bfloat16)
    token_grad = (jnp.dot(d_gate, gate_weight.T, preferred_element_type=jnp.float32)
                  + jnp.dot(d_up, up_weight.T, preferred_element_type=jnp.float32)).astype(jnp.bfloat16)
    return ffn_output, token_grad, gate_grad, up_grad, down_grad
```

```python
import functools

import jax
import jax.numpy as jnp
from jax import lax
from jax.experimental import pallas as pl
from jax.experimental.pallas import tpu as pltpu
from jax.sharding import PartitionSpec as P

F32 = jnp.float32
BF16 = jnp.bfloat16
VMEM_BYTES = 48 * 1024 * 1024


def dot(a, b, ca, cb):
    return lax.dot_general(a, b, (((ca,), (cb,)), ((), ())), preferred_element_type=F32)


def params():
    return pltpu.CompilerParams(vmem_limit_bytes=VMEM_BYTES)


def order_kernel(mask_ref, tokens_ref, upstream_ref, one_hot_ref, tokens_out, grad_out):
    tok = tokens_ref.shape[0]
    live = grad_out.shape[1]
    mask = mask_ref[...].astype(F32)
    before = lax.broadcasted_iota(jnp.int32, (tok, tok), 0) < lax.broadcasted_iota(jnp.int32, (tok, tok), 1)
    rank = dot(jnp.broadcast_to(mask, (8, tok)).astype(BF16), before.astype(F32).astype(BF16), 1, 0)[:1]
    column = lax.broadcasted_iota(jnp.int32, (1, tok), 1).astype(F32)
    place = jnp.where(mask > 0, rank, live + column - rank)
    row = lax.broadcasted_iota(jnp.int32, (tok, tok), 0).astype(F32)
    one_hot = (row == place).astype(F32).astype(BF16)
    one_hot_ref[...] = one_hot
    tokens_out[...] = dot(tokens_ref[...], one_hot, 0, 1).astype(BF16)
    grad_out[...] = dot(upstream_ref[...], one_hot[:live], 0, 1).astype(BF16)


def order_tokens(tokens, upstream, loss_mask, live):
    tok, width = tokens.shape

    def whole(*shape):
        return pl.BlockSpec(shape, lambda i: (0, 0))

    return pl.pallas_call(
        order_kernel,
        grid=(1,),
        in_specs=[whole(1, tok), whole(tok, width), whole(tok, width)],
        out_specs=[whole(tok, tok), whole(width, tok), whole(width, live)],
        out_shape=(
            jax.ShapeDtypeStruct((tok, tok), BF16),
            jax.ShapeDtypeStruct((width, tok), BF16),
            jax.ShapeDtypeStruct((width, live), BF16),
        ),
        compiler_params=params(),
        name="order_tokens",
    )(loss_mask.reshape(1, tok), tokens, upstream)


def pair_of(mine, other, core):
    return jnp.concatenate([jnp.where(core == 0, mine, other), jnp.where(core == 0, other, mine)], axis=0)


def forward_first_kernel(where_ref, mine, other, gate_w, up_w, gate_acc, up_acc):
    x = pair_of(mine[0], other[0], where_ref[0])

    @pl.when(pl.program_id(0) == 0)
    def _():
        gate_acc[...] = dot(gate_w[...], x, 1, 0)
        up_acc[...] = dot(up_w[...], x, 1, 0)

    @pl.when(pl.program_id(0) > 0)
    def _():
        gate_acc[...] += dot(gate_w[...], x, 1, 0)
        up_acc[...] += dot(up_w[...], x, 1, 0)


def forward_rest_kernel(
    live, where_ref, mine, other, gate_w, up_w, gate_in, up_in, hidden_ref, hidden_t_ref, act_ref, slope_ref, gate_acc, up_acc
):
    x = pair_of(mine[0], other[0], where_ref[0])

    @pl.when(pl.program_id(0) == 0)
    def _():
        gate_acc[...] = gate_in[...] + dot(gate_w[...], x, 1, 0)
        up_acc[...] = up_in[...] + dot(up_w[...], x, 1, 0)

    @pl.when(pl.program_id(0) > 0)
    def _():
        gate_acc[...] += dot(gate_w[...], x, 1, 0)
        up_acc[...] += dot(up_w[...], x, 1, 0)

    @pl.when(pl.program_id(0) == pl.num_programs(0) - 1)
    def _():
        gate_lin = gate_acc[...]
        up_lin = up_acc[...]
        sig = jax.nn.sigmoid(gate_lin)
        act = gate_lin * sig
        hidden = (act * up_lin).astype(BF16)
        hidden_ref[...] = hidden.T
        hidden_t_ref[...] = hidden[:, :live]
        act_ref[...] = act[:, :live]
        slope_ref[...] = (up_lin * sig * (1.0 + gate_lin * (1.0 - sig)))[:, :live]


def whole(*shape):
    return pl.BlockSpec(shape, lambda j, s: (0, 0))


def stacked(*shape):
    return pl.BlockSpec((1, *shape), lambda j, s: (j, 0, 0))


def columns(ff, width):
    return pl.BlockSpec((ff, 2 * width), lambda j, s: (0, s[1 + j]))


def call(kernel, name, where, operands, in_specs, outs, out_specs, flops, nbytes, scratch=()):
    return pl.pallas_call(
        kernel,
        grid_spec=pltpu.PrefetchScalarGridSpec(
            num_scalar_prefetch=1,
            grid=(where.shape[0] - 1,),
            in_specs=in_specs,
            out_specs=out_specs,
            scratch_shapes=scratch,
        ),
        out_shape=[jax.ShapeDtypeStruct(shape, kind) for shape, kind in outs],
        compiler_params=params(),
        cost_estimate=pl.CostEstimate(flops=flops, bytes_accessed=nbytes, transcendentals=0),
        name=name,
    )(where, *operands)


def forward_first(where, mine, other, gate_w, up_w):
    steps, width, tok = mine.shape
    ff = gate_w.shape[0]
    return call(
        forward_first_kernel,
        "forward_first",
        where,
        (mine, other, gate_w, up_w),
        [stacked(width, tok), stacked(width, tok), columns(ff, width), columns(ff, width)],
        [((ff, tok), F32), ((ff, tok), F32)],
        [whole(ff, tok), whole(ff, tok)],
        8 * steps * width * ff * tok,
        8 * steps * width * ff,
    )


def forward_rest(where, mine, other, gate_w, up_w, gate_acc, up_acc, live):
    steps, width, tok = mine.shape
    ff = gate_w.shape[0]
    return call(
        functools.partial(forward_rest_kernel, live),
        "forward_rest",
        where,
        (mine, other, gate_w, up_w, gate_acc, up_acc),
        [
            stacked(width, tok),
            stacked(width, tok),
            columns(ff, width),
            columns(ff, width),
            whole(ff, tok),
            whole(ff, tok),
        ],
        [((tok, ff), BF16), ((ff, live), BF16), ((ff, live), F32), ((ff, live), F32)],
        [whole(tok, ff), whole(ff, live), whole(ff, live), whole(ff, live)],
        8 * steps * width * ff * tok,
        8 * steps * width * ff,
        [pltpu.VMEM((ff, tok), F32), pltpu.VMEM((ff, tok), F32)],
    )


def down_kernel(
    where_ref, hidden, act, slope, mine, other, down_w, keep_ref, send_ref, d_gate_ref, d_up_ref, d_gate_t_ref, d_up_t_ref, d_hidden
):
    core = where_ref[0]
    w = down_w[...]
    width = mine.shape[1]
    out = dot(hidden[...], w, 1, 0)
    low, high = out[:, :width], out[:, width:]
    keep_ref[0] = jnp.where(core == 0, low, high)
    send_ref[0] = jnp.where(core == 0, high, low).astype(BF16)
    part = dot(w, pair_of(mine[0], other[0], core), 1, 0)

    @pl.when(pl.program_id(0) == 0)
    def _():
        d_hidden[...] = part

    @pl.when(pl.program_id(0) > 0)
    def _():
        d_hidden[...] += part

    @pl.when(pl.program_id(0) == pl.num_programs(0) - 1)
    def _():
        d_up = (d_hidden[...] * act[...]).astype(BF16)
        d_gate = (d_hidden[...] * slope[...]).astype(BF16)
        d_up_t_ref[...] = d_up
        d_gate_t_ref[...] = d_gate
        d_up_ref[...] = d_up.T
        d_gate_ref[...] = d_gate.T


def down(where, hidden, act, slope, mine, other, down_w):
    steps, width, live = mine.shape
    tok, ff = hidden.shape
    return call(
        down_kernel,
        "down",
        where,
        (hidden, act, slope, mine, other, down_w),
        [whole(tok, ff), whole(ff, live), whole(ff, live), stacked(width, live), stacked(width, live), columns(ff, width)],
        [((steps, tok, width), F32), ((steps, tok, width), BF16)] + 2 * [((live, ff), BF16)] + 2 * [((ff, live), BF16)],
        [stacked(tok, width), stacked(tok, width), whole(live, ff), whole(live, ff), whole(ff, live), whole(ff, live)],
        2 * (tok + live) * down_w.size,
        2 * down_w.size,
        [pltpu.VMEM((ff, live), F32)],
    )


def token_grad_kernel(where_ref, d_gate, d_up, gate_w, up_w, keep_ref, send_ref):
    core = where_ref[0]
    width = keep_ref.shape[2]
    out = dot(d_gate[...], gate_w[...], 1, 0) + dot(d_up[...], up_w[...], 1, 0)
    low, high = out[:, :width], out[:, width:]
    keep_ref[0] = jnp.where(core == 0, low, high)
    send_ref[0] = jnp.where(core == 0, high, low).astype(BF16)


def token_grad_parts(where, d_gate, d_up, gate_w, up_w, width):
    live, ff = d_gate.shape
    steps = where.shape[0] - 1
    return call(
        token_grad_kernel,
        "token_grad_parts",
        where,
        (d_gate, d_up, gate_w, up_w),
        [whole(live, ff), whole(live, ff), columns(ff, width), columns(ff, width)],
        [((steps, live, width), F32), ((steps, live, width), BF16)],
        [stacked(live, width), stacked(live, width)],
        8 * live * steps * ff * width,
        8 * steps * ff * width,
    )


def weight_grad_kernel(where_ref, hid, mine, other, out_ref):
    x = pair_of(mine[0], other[0], where_ref[0])
    out_ref[...] = dot(hid[...], x, 1, 1).astype(BF16)


def weight_grad(where, hid, mine, other, name):
    steps, width, _ = mine.shape
    ff, live = hid.shape
    return call(
        weight_grad_kernel,
        name,
        where,
        (hid, mine, other),
        [whole(ff, live), stacked(width, live), stacked(width, live)],
        [((ff, 2 * steps * width), BF16)],
        [columns(ff, width)],
        4 * live * ff * steps * width,
        4 * ff * steps * width,
    )[0]


def last_kernel(one_hot, *refs):
    total = refs[0][...].astype(F32)
    for part in refs[1:-1]:
        total = total + part[...].astype(F32)
    refs[-1][...] = dot(one_hot[...], total.astype(BF16), 0, 0).astype(BF16)


def last_sum(one_hot, parts, name):
    rows, tok = one_hot.shape
    return pl.pallas_call(
        last_kernel,
        out_shape=jax.ShapeDtypeStruct((tok, parts[0].shape[1]), BF16),
        compiler_params=params(),
        name=name,
    )(one_hot, *parts)


def flip(x, bits):
    return lax.ppermute(x, "hid", [(i, i ^ bits) for i in range(16)])


def gather(x):
    z2 = flip(x, 8)
    z1 = flip(x, 4)
    y = flip(x, 2)
    z3 = flip(z2, 4)
    first = jnp.stack([x, y, z1, flip(z1, 2)])
    rest = jnp.stack([z2, flip(z2, 2), z3, flip(z3, 2)])
    return first, flip(first, 1), rest, flip(rest, 1)


def scatter_sum(keep, send):
    recv = flip(send, 1)
    pair = keep + recv.astype(F32)
    row = [None] * 4
    for k in (3, 2, 1, 0):
        row[k] = pair[2 * k] + flip(pair[2 * k + 1].astype(BF16), 2).astype(F32)
    two = row[2] + flip(row[3].astype(BF16), 4).astype(F32)
    return row[0], flip(two.astype(BF16), 8), flip(row[1].astype(BF16), 4)


def body16(tokens, upstream, loss_mask, gate_weight, up_weight, down_weight):
    live = tokens.shape[0] // 2
    width = tokens.shape[1]
    me = lax.axis_index("hid")
    chips = (me // 2) ^ jnp.arange(8)
    where = jnp.concatenate([(me % 2)[None], chips]).astype(jnp.int32)
    where_first, where_rest = where[:5], jnp.concatenate([where[:1], where[5:]])
    gate_w, up_w = gate_weight.T, up_weight.T
    one_hot, tokens, grad = order_tokens(tokens, upstream, loss_mask, live)
    x_first, x_first_other, x_rest, x_rest_other = gather(tokens)
    g_first, g_first_other, g_rest, g_rest_other = gather(grad)
    acc = forward_first(where_first, x_first, x_first_other, gate_w, up_w)
    hidden, hidden_t, act, slope = forward_rest(where_rest, x_rest, x_rest_other, gate_w, up_w, *acc, live)
    x_mine, x_other = jnp.concatenate([x_first, x_rest]), jnp.concatenate([x_first_other, x_rest_other])
    g_mine, g_other = jnp.concatenate([g_first, g_rest]), jnp.concatenate([g_first_other, g_rest_other])
    out_keep, out_send, d_gate, d_up, d_gate_t, d_up_t = down(where, hidden, act, slope, g_mine, g_other, down_weight)
    out_parts = scatter_sum(out_keep, out_send)
    tg_keep, tg_send = token_grad_parts(where, d_gate, d_up, gate_w, up_w, width)
    tg_parts = scatter_sum(tg_keep, tg_send)
    down_grad = weight_grad(where, hidden_t, g_mine, g_other, "down_grad")
    gate_grad = weight_grad(where, d_gate_t, x_mine, x_other, "gate_grad").T
    up_grad = weight_grad(where, d_up_t, x_mine, x_other, "up_grad").T
    ffn_output = last_sum(one_hot, out_parts, "ffn_output")
    token_grad = last_sum(one_hot[:live], tg_parts, "token_grad")
    return ffn_output, token_grad, gate_grad, up_grad, down_grad


def body_any(tokens, upstream, loss_mask, gate_weight, up_weight, down_weight):
    masked = upstream * loss_mask[:, None].astype(upstream.dtype)
    tokens = lax.all_gather(tokens, "hid", axis=1, tiled=True)
    grad = lax.all_gather(masked, "hid", axis=1, tiled=True)
    gate_lin = dot(tokens, gate_weight, 1, 0)
    up_lin = dot(tokens, up_weight, 1, 0)
    sig = jax.nn.sigmoid(gate_lin)
    act = gate_lin * sig
    hidden = (act * up_lin).astype(BF16)
    out = lax.psum_scatter(dot(down_weight, hidden, 0, 1), "hid", scatter_dimension=0, tiled=True)
    d_hidden = dot(grad, down_weight, 1, 1)
    d_up = (d_hidden * act).astype(BF16)
    d_gate = (d_hidden * up_lin * sig * (1.0 + gate_lin * (1.0 - sig))).astype(BF16)
    down_grad = dot(hidden, grad, 0, 0).astype(BF16)
    gate_grad = dot(tokens, d_gate, 0, 0).astype(BF16)
    up_grad = dot(tokens, d_up, 0, 0).astype(BF16)
    back = dot(gate_weight, d_gate, 1, 1) + dot(up_weight, d_up, 1, 1)
    back = lax.psum_scatter(back, "hid", scatter_dimension=0, tiled=True)
    return out.T.astype(BF16), back.T.astype(BF16), gate_grad, up_grad, down_grad


def solution(mesh):
    spec = P("groups", "hid")
    in_specs = (spec, spec, P("groups"), P(None, "hid"), P(None, "hid"), P("hid", None))
    out_specs = (spec, spec, spec, spec, P("hid", "groups"))
    body = body16 if mesh.shape["hid"] == 16 else body_any
    return jax.shard_map(body, mesh=mesh, in_specs=in_specs, out_specs=out_specs, check_vma=False)
```

```python
import functools

import jax
import jax.numpy as jnp
from jax import lax
from jax.experimental import pallas as pl
from jax.experimental.pallas import tpu as pltpu
from jax.sharding import PartitionSpec as P

F32 = jnp.float32
BF16 = jnp.bfloat16
VMEM_BYTES = 52 * 1024 * 1024


def dot(a, b, ca, cb):
    return lax.dot_general(a, b, (((ca,), (cb,)), ((), ())), preferred_element_type=F32)


def params():
    return pltpu.CompilerParams(vmem_limit_bytes=VMEM_BYTES)


def my_core():
    return lax.axis_index("hid") % 2


def chip_columns(k, width):
    chip = (lax.axis_index("hid") // 2) ^ k
    return pl.ds(pl.multiple_of(chip * (2 * width), 2 * width), 2 * width)


def call(kernel, name, operands, outs, scratch, flops, nbytes, alias=None):
    return pl.pallas_call(
        kernel,
        in_specs=[pl.BlockSpec(memory_space=pl.ANY)] * len(operands),
        out_specs=[pl.BlockSpec(memory_space=pl.ANY)] * len(outs),
        out_shape=[jax.ShapeDtypeStruct(shape, kind) for shape, kind in outs],
        scratch_shapes=scratch,
        input_output_aliases={} if alias is None else {alias: 0},
        compiler_params=params(),
        cost_estimate=pl.CostEstimate(flops=flops, bytes_accessed=nbytes, transcendentals=0),
        name=name,
    )(*operands)


def copies(sems, *pairs):
    made = [pltpu.make_async_copy(src, dst, sems.at[i]) for i, (src, dst) in enumerate(pairs)]
    for c in made:
        c.start()
    return made


def wait_all(made):
    for c in made:
        c.wait()


def dma(count):
    return pltpu.SemaphoreType.DMA((count,))


def start_each(steps, make):
    def one(j, carry):
        make(j).start()
        return carry

    lax.fori_loop(0, steps, one, 0)


def wait_each(steps, make):
    def one(j, carry):
        make(j).wait()
        return carry

    lax.fori_loop(0, steps, one, 0)


def each(steps, body):
    def one(j, carry):
        body(j)
        return carry

    lax.fori_loop(0, steps, one, 0)


def stream(steps, ahead, make, body):
    for j in range(min(ahead, steps)):
        make(j).start()

    def one(j):
        make(j).wait()

        @pl.when(j + ahead < steps)
        def _():
            make(j + ahead).start()

        body(j)

    each(steps, one)


def order_kernel(
    mask_ref, tokens_ref, upstream_ref, one_hot_ref, tokens_out, grad_out, mask_v, tokens_v, upstream_v, one_hot_v, out_v, grad_v, sems
):
    made = copies(sems, (mask_ref, mask_v), (tokens_ref, tokens_v), (upstream_ref, upstream_v))
    tok = tokens_v.shape[0]
    live = tok // 2
    made[0].wait()
    mask = mask_v[...].astype(F32)
    before = lax.broadcasted_iota(jnp.int32, (tok, tok), 0) < lax.broadcasted_iota(jnp.int32, (tok, tok), 1)
    rank = dot(jnp.broadcast_to(mask, (8, tok)).astype(BF16), before.astype(F32).astype(BF16), 1, 0)[:1]
    column = lax.broadcasted_iota(jnp.int32, (1, tok), 1).astype(F32)
    place = jnp.where(mask > 0, rank, live + column - rank)
    row = lax.broadcasted_iota(jnp.int32, (tok, tok), 0).astype(F32)
    one_hot = (row == place).astype(F32).astype(BF16)
    one_hot_v[...] = one_hot
    made[1].wait()
    out_v[...] = dot(tokens_v[...], one_hot, 0, 1).astype(BF16)
    made[2].wait()
    out = copies(sems, (one_hot_v, one_hot_ref), (out_v, tokens_out))
    grad_v[...] = dot(upstream_v[...], one_hot[:live], 0, 1).astype(BF16)
    wait_all(out + copies(sems.at[pl.ds(2, 1)], (grad_v, grad_out)))


def order_tokens(tokens, upstream, loss_mask):
    tok, width = tokens.shape
    outs = [((tok, tok), BF16), ((width, tok), BF16), ((width, tok // 2), BF16)]
    return call(
        order_kernel,
        "order_tokens",
        (loss_mask.reshape(1, tok), tokens, upstream),
        outs,
        [
            pltpu.VMEM((1, tok), jnp.int32),
            pltpu.VMEM((tok, width), BF16),
            pltpu.VMEM((tok, width), BF16),
            *[pltpu.VMEM(*out) for out in outs],
            dma(3),
        ],
        3 * tok * tok * width,
        8 * tok * width,
    )


def pair_copies(mine, other, dst):
    width = mine.shape[1]
    core = my_core()
    return (
        (mine, dst.at[:, pl.ds(pl.multiple_of(core * width, width), width)]),
        (other, dst.at[:, pl.ds(pl.multiple_of((1 - core) * width, width), width)]),
    )


def row_columns(k, wide):
    row = (lax.axis_index("hid") // 4) ^ k
    return pl.ds(pl.multiple_of(row * wide, wide), wide)


def row_copies(mine, other, dst):
    rows, wide, _ = dst.shape
    width = wide // 4
    in_row = lax.axis_index("hid") % 4
    pairs = []
    for row in range(rows):
        for side in range(2):
            for flipped, part in enumerate((mine, other)):
                at = pl.ds(pl.multiple_of((in_row ^ (2 * side + flipped)) * width, width), width)
                pairs.append((part.at[2 * row + side], dst.at[row, at]))
    return pairs


def piece_copies(sems, total, rounded, keep_ref, send_ref):
    rows, _, wide = total.shape
    width = wide // 4
    in_row = lax.axis_index("hid") % 4
    pairs = []
    for row in range(rows):
        for side in range(2):
            at = [pl.ds(pl.multiple_of((in_row ^ (2 * side + i)) * width, width), width) for i in range(2)]
            pairs.append((total.at[row, :, at[0]], keep_ref.at[2 * row + side]))
            pairs.append((rounded.at[row, :, at[1]], send_ref.at[2 * row + side]))
    return copies(sems, *pairs)


def start_gate_up(gate_w, up_w, base, j, buffer, sem):
    wide = buffer.shape[1]
    for i, weight in enumerate((gate_w, up_w)):

        @pl.when(j % 2 == i)
        def _():
            pltpu.make_async_copy(weight.at[:, row_columns(base + j // 2, wide)], buffer, sem).start()


def start_down(down_w, j, buffer, sem):
    pltpu.make_async_copy(down_w.at[:, row_columns(j, buffer.shape[1])], buffer, sem).start()


def wait_block(down_w, buffer, sem):
    pltpu.make_async_copy(down_w.at[:, pl.ds(0, buffer.shape[1])], buffer, sem).wait()


def forward_kernel(
    mine, other, gate_w, up_w, down_w, hidden_t_ref, act_ref, slope_ref, keep_ref, send_ref, x, w, acc, *rest
):
    hidden_v, hidden_t_v, act_v, slope_v, total, rounded, sems, x_sems, w_sems, out_sems = rest
    slots = w.shape[0]
    rows = x.shape[0]
    steps = 2 * rows

    def start(j):
        slot = j % slots
        start_gate_up(gate_w, up_w, 0, j, w.at[slot], w_sems.at[slot])

    def start_last(j):
        start_down(down_w, j, w.at[j % slots], w_sems.at[j % slots])

    x_in = copies(x_sems, *row_copies(mine, other, x))
    start(0)
    start(1)
    acc[...] = jnp.zeros_like(acc)
    wait_all(x_in)

    def one(j):
        slot = j % slots
        wait_block(gate_w, w.at[slot], w_sems.at[slot])

        @pl.when(j + 2 < steps)
        def _():
            start(j + 2)

        @pl.when(j + 2 >= steps)
        def _():
            start_last(j + 2 - steps)

        acc[j % 2] += dot(w[slot], x[j // 2], 1, 0)

    each(steps, one)
    live = act_v.shape[1]
    gate_lin = acc[0]
    up_lin = acc[1]
    sig = jax.nn.sigmoid(gate_lin)
    act = gate_lin * sig
    hidden = (act * up_lin).astype(BF16)
    hidden_t_v[...] = hidden[:, :live]
    act_v[...] = act[:, :live]
    slope_v[...] = (up_lin * sig * (1.0 + gate_lin * (1.0 - sig)))[:, :live]
    hidden_v[...] = hidden.T
    out = copies(sems, (hidden_t_v, hidden_t_ref), (act_v, act_ref), (slope_v, slope_ref))

    def two(j):
        slot = j % slots
        wait_block(down_w, w.at[slot], w_sems.at[slot])

        @pl.when(j + 2 < rows)
        def _():
            start_last(j + 2)

        part = dot(hidden_v[...], w[slot], 1, 0)
        total[j] = part
        rounded[j] = part.astype(BF16)

    each(rows, two)
    wait_all(out + piece_copies(out_sems, total, rounded, keep_ref, send_ref))


def forward(mine, other, gate_w, up_w, down_w, live):
    chips, width, tok = mine.shape
    ff = gate_w.shape[0]
    rows, slots = chips // 2, 4
    return call(
        forward_kernel,
        "forward",
        (mine, other, gate_w, up_w, down_w),
        [
            ((ff, live), BF16),
            ((ff, live), F32),
            ((ff, live), F32),
            ((chips, tok, width), F32),
            ((chips, tok, width), BF16),
        ],
        [
            pltpu.VMEM((rows, 4 * width, tok), BF16),
            pltpu.VMEM((slots, ff, 4 * width), BF16),
            pltpu.VMEM((2, ff, tok), F32),
            pltpu.VMEM((tok, ff), BF16),
            pltpu.VMEM((ff, live), BF16),
            pltpu.VMEM((ff, live), F32),
            pltpu.VMEM((ff, live), F32),
            pltpu.VMEM((rows, tok, 4 * width), F32),
            pltpu.VMEM((rows, tok, 4 * width), BF16),
            dma(3),
            dma(2 * chips),
            dma(slots),
            dma(2 * chips),
        ],
        12 * chips * width * ff * tok,
        12 * chips * width * ff,
    )


def token_grad_loop(base, gate_w, up_w, d_hid, w, total, rounded, w_sems):
    steps = w.shape[0]
    total[...] = jnp.zeros_like(total)

    def one(j):
        wait_block(gate_w, w.at[j], w_sems.at[j])

        @pl.when(j + 2 < steps)
        def _():
            start_gate_up(gate_w, up_w, base, j + 2, w.at[j + 2], w_sems.at[j + 2])

        part = total[j // 2] + dot(d_hid[j % 2], w[j], 1, 0)
        total[j // 2] = part
        rounded[j // 2] = part.astype(BF16)

    each(steps, one)


def backward_first_kernel(
    base, mine, other, act_ref, slope_ref, gate_w, up_w, down_w, d_hid_ref, d_hid_t_ref, keep_ref, send_ref, g, act, slope, *rest
):
    w, acc, d_hid, d_hid_t, total, rounded, sems, g_sems, w_sems, t_sems, out_sems = rest
    steps = w.shape[0]
    first = copies(g_sems, *row_copies(mine, other, g))
    for j in range(2):
        start_down(down_w, j, w.at[j], w_sems.at[j])
    late = copies(sems, (act_ref, act), (slope_ref, slope))
    acc[...] = jnp.zeros_like(acc)
    wait_all(first)

    def one(j):
        wait_block(down_w, w.at[j], w_sems.at[j])

        @pl.when(j + 2 < steps)
        def _():
            start_down(down_w, j + 2, w.at[j + 2], w_sems.at[j + 2])

        acc[...] += dot(w[j], g[j], 1, 0)

        @pl.when(j + 2 >= steps)
        def _():
            start_gate_up(gate_w, up_w, base, j + 2 - steps, w.at[j + 2 - steps], t_sems.at[j + 2 - steps])

    each(steps, one)
    wait_all(late)
    d_gate = (acc[...] * slope[...]).astype(BF16)
    d_up = (acc[...] * act[...]).astype(BF16)
    d_hid_t[0] = d_gate
    d_hid_t[1] = d_up
    d_hid[0] = d_gate.T
    d_hid[1] = d_up.T
    out = copies(sems, (d_hid, d_hid_ref), (d_hid_t, d_hid_t_ref))
    token_grad_loop(base, gate_w, up_w, d_hid, w, total, rounded, t_sems)
    wait_all(out + piece_copies(out_sems, total, rounded, keep_ref, send_ref))


def backward_first(base, mine, other, act, slope, gate_w, up_w, down_w):
    chips, width, live = mine.shape
    ff = act.shape[0]
    rows = chips // 2
    steps = rows
    d_hid, d_hid_t = ((2, live, ff), BF16), ((2, ff, live), BF16)
    return call(
        functools.partial(backward_first_kernel, base),
        "backward_first",
        (mine, other, act, slope, gate_w, up_w, down_w),
        [d_hid, d_hid_t, ((steps, live, width), F32), ((steps, live, width), BF16)],
        [
            pltpu.VMEM((rows, 4 * width, live), BF16),
            pltpu.VMEM((ff, live), F32),
            pltpu.VMEM((ff, live), F32),
            pltpu.VMEM((steps, ff, 4 * width), BF16),
            pltpu.VMEM((ff, live), F32),
            pltpu.VMEM(*d_hid),
            pltpu.VMEM(*d_hid_t),
            pltpu.VMEM((steps // 2, live, 4 * width), F32),
            pltpu.VMEM((steps // 2, live, 4 * width), BF16),
            dma(2),
            dma(2 * chips),
            dma(steps),
            dma(steps),
            dma(2 * steps),
        ],
        4 * live * down_w.size,
        4 * down_w.size,
    )


def backward_rest_kernel(base, d_hid_ref, gate_w, up_w, keep_ref, send_ref, d_hid, w, total, rounded, sems, w_sems, out_sems):
    first = copies(sems, (d_hid_ref, d_hid))
    for j in range(2):
        start_gate_up(gate_w, up_w, base, j, w.at[j], w_sems.at[j])
    wait_all(first)
    token_grad_loop(base, gate_w, up_w, d_hid, w, total, rounded, w_sems)
    wait_all(piece_copies(out_sems, total, rounded, keep_ref, send_ref))


def backward_rest(base, steps, d_hid, gate_w, up_w, width):
    _, live, ff = d_hid.shape
    return call(
        functools.partial(backward_rest_kernel, base),
        "backward_rest",
        (d_hid, gate_w, up_w),
        [((steps, live, width), F32), ((steps, live, width), BF16)],
        [
            pltpu.VMEM((2, live, ff), BF16),
            pltpu.VMEM((steps, ff, 4 * width), BF16),
            pltpu.VMEM((steps // 2, live, 4 * width), F32),
            pltpu.VMEM((steps // 2, live, 4 * width), BF16),
            dma(1),
            dma(steps),
            dma(2 * steps),
        ],
        8 * live * steps * ff * width,
        8 * steps * ff * width,
    )


def weight_grad_kernel(which, hid_ref, mine, other, *refs):
    out_ref, hid, x, out_v, sems, out_sems = refs[-6:]
    steps = x.shape[0]
    width = mine.shape[1]
    live = hid.shape[1]
    parts = [part.at[:, :, pl.ds(0, live)] for part in (mine, other)]
    source = hid_ref if which is None else hid_ref.at[which]
    wait_all(copies(sems, (source, hid), *pair_copies(*parts, x)))

    def out_copy(j):
        return pltpu.make_async_copy(out_v.at[j], out_ref.at[:, chip_columns(j, width)], out_sems.at[j])

    def step(j):
        out_v[j] = dot(hid[...], x[j], 1, 1).astype(BF16)
        out_copy(j).start()

    each(steps, step)
    wait_each(steps, out_copy)


def weight_grad(hid, which, mine, other, name):
    steps, width, _ = mine.shape
    ff, live = hid.shape[-2:]
    return call(
        functools.partial(weight_grad_kernel, which),
        name,
        (hid, mine, other),
        [((ff, 2 * steps * width), BF16)],
        [
            pltpu.VMEM((ff, live), BF16),
            pltpu.VMEM((steps, 2 * width, live), BF16),
            pltpu.VMEM((steps, ff, 2 * width), BF16),
            dma(3),
            dma(steps),
        ],
        4 * live * ff * steps * width,
        4 * ff * steps * width,
    )[0]


def last_kernel(one_hot, *refs):
    total = refs[0][...].astype(F32)
    for part in refs[1:-1]:
        total = total + part[...].astype(F32)
    refs[-1][...] = dot(one_hot[...], total.astype(BF16), 0, 0).astype(BF16)


def last_sum(one_hot, parts, name):
    return pl.pallas_call(
        last_kernel,
        out_shape=jax.ShapeDtypeStruct((one_hot.shape[1], parts[0].shape[1]), BF16),
        compiler_params=params(),
        name=name,
    )(one_hot, *parts)


def flip(x, bits):
    return lax.ppermute(x, "hid", [(i, i ^ bits) for i in range(16)])


def plus(a, b):
    return a.astype(F32) + b.astype(F32)


def join(*arrays):
    return lax.optimization_barrier(arrays)


def body16(tokens, upstream, loss_mask, gate_weight, up_weight, down_weight):
    tok, width = tokens.shape
    live = tok // 2
    gate_w, up_w = gate_weight.T, up_weight.T
    one_hot, x, g = order_tokens(tokens, upstream, loss_mask)
    z2, z1, y = flip(x, 8), flip(x, 4), flip(x, 2)
    gz1, gy = flip(g, 4), flip(g, 2)
    z2, z1, y, gz1, gy, g = join(z2, z1, y, gz1, gy, g)
    z3, yz1, yz2 = flip(z2, 4), flip(z1, 2), flip(z2, 2)
    gz2 = flip(g, 8)
    z3, yz1, yz2, gz2, gz1 = join(z3, yz1, yz2, gz2, gz1)
    yz3 = flip(z3, 2)
    most = jnp.stack([x, y, z1, yz1, z2, yz2, z3])
    most_other = flip(most, 1)
    gz3, gyz1, gyz2 = flip(gz2, 4), flip(gz1, 2), flip(gz2, 2)
    most_other, yz3, gz3, gyz1, gyz2 = join(most_other, yz3, gz3, gyz1, gyz2)
    x_mine = jnp.concatenate([most, yz3[None]])
    x_other = jnp.concatenate([most_other, flip(yz3, 1)[None]])
    gyz3 = flip(gz3, 2)
    g_most = jnp.stack([g, gy, gz1, gyz1, gz2, gyz2, gz3])
    g_most_other = flip(g_most, 1)
    hidden_t, act, slope, out_keep, out_send = forward(x_mine, x_other, gate_w, up_w, down_weight, live)
    out_send, gyz3, g_most_other = join(out_send, gyz3, g_most_other)
    g_mine = jnp.concatenate([g_most, gyz3[None]])
    g_other = jnp.concatenate([g_most_other, flip(gyz3, 1)[None]])
    recv = flip(out_send, 1)
    d_hid, d_hid_t, tk1, ts1 = backward_first(2, g_mine, g_other, act, slope, gate_w, up_w, down_weight)
    d_hid, recv, ts1 = join(d_hid, recv, ts1)
    y23 = flip(plus(out_keep[5::2], recv[5::2]).astype(BF16), 2)
    recv1 = flip(ts1, 1)
    tk0, ts0 = backward_rest(0, 4, d_hid, gate_w, up_w, width)
    ts0, y23, recv1, recv, hidden_t = join(ts0, y23, recv1, recv, hidden_t)
    z13 = flip((plus(out_keep[6], recv[6]) + y23[1].astype(F32)).astype(BF16), 4)
    y01 = jnp.concatenate([plus(out_keep[1:4:2], recv[1:4:2]), plus(tk1[1::2], recv1[1::2])], axis=1)
    y01 = flip(y01.astype(BF16), 2)
    recv0 = flip(ts0, 1)
    down_grad = weight_grad(hidden_t, None, g_mine, g_other, "down_grad")
    down_grad, z13, y01, recv0, d_hid_t = join(down_grad, z13, y01, recv0, d_hid_t)
    y01, ty1 = y01[:, :tok], y01[:, tok:]
    z2 = flip((plus(out_keep[4], recv[4]) + plus(y23[0], z13)).astype(BF16), 8)
    z1 = jnp.concatenate([plus(out_keep[2], recv[2]) + y01[1].astype(F32), plus(tk1[2], recv1[2]) + ty1[1].astype(F32)])
    z1 = flip(z1.astype(BF16), 4)
    ty0 = flip(plus(tk0[1::2], recv0[1::2]).astype(BF16), 2)
    gate_grad = weight_grad(d_hid_t, 0, x_mine, x_other, "gate_grad")
    gate_grad, d_hid_t, ty0, z2, z1 = join(gate_grad, d_hid_t, ty0, z2, z1)
    z1, tz13 = z1[:tok], z1[tok:]
    tz2 = flip((plus(tk1[0], recv1[0]) + plus(ty1[0], tz13)).astype(BF16), 8)
    tz1 = flip((plus(tk0[2], recv0[2]) + ty0[1].astype(F32)).astype(BF16), 4)
    ffn_output = last_sum(one_hot, (plus(out_keep[0], recv[0]) + y01[0].astype(F32), z2, z1), "ffn_output")
    up_grad = weight_grad(d_hid_t, 1, x_mine, x_other, "up_grad")
    up_grad, tz2, tz1 = join(up_grad, tz2, tz1)
    token_grad = last_sum(one_hot[:live], (plus(tk0[0], recv0[0]) + ty0[0].astype(F32), tz2, tz1), "token_grad")
    return ffn_output, token_grad, gate_grad.T, up_grad.T, down_grad


def body_any(tokens, upstream, loss_mask, gate_weight, up_weight, down_weight):
    masked = upstream * loss_mask[:, None].astype(upstream.dtype)
    tokens = lax.all_gather(tokens, "hid", axis=1, tiled=True)
    grad = lax.all_gather(masked, "hid", axis=1, tiled=True)
    gate_lin = dot(tokens, gate_weight, 1, 0)
    up_lin = dot(tokens, up_weight, 1, 0)
    sig = jax.nn.sigmoid(gate_lin)
    act = gate_lin * sig
    hidden = (act * up_lin).astype(BF16)
    out = lax.psum_scatter(dot(down_weight, hidden, 0, 1), "hid", scatter_dimension=0, tiled=True)
    d_hidden = dot(grad, down_weight, 1, 1)
    d_up = (d_hidden * act).astype(BF16)
    d_gate = (d_hidden * up_lin * sig * (1.0 + gate_lin * (1.0 - sig))).astype(BF16)
    down_grad = dot(hidden, grad, 0, 0).astype(BF16)
    gate_grad = dot(tokens, d_gate, 0, 0).astype(BF16)
    up_grad = dot(tokens, d_up, 0, 0).astype(BF16)
    back = dot(gate_weight, d_gate, 1, 1) + dot(up_weight, d_up, 1, 1)
    back = lax.psum_scatter(back, "hid", scatter_dimension=0, tiled=True)
    return out.T.astype(BF16), back.T.astype(BF16), gate_grad, up_grad, down_grad


def solution(mesh):
    spec = P("groups", "hid")
    in_specs = (spec, spec, P("groups"), P(None, "hid"), P(None, "hid"), P("hid", None))
    out_specs = (spec, spec, spec, spec, P("hid", "groups"))
    body = body16 if mesh.shape["hid"] == 16 else body_any
    return jax.shard_map(body, mesh=mesh, in_specs=in_specs, out_specs=out_specs, check_vma=False)
```

```python
import functools

import jax
import jax.numpy as jnp
from jax import lax
from jax.experimental import pallas as pl
from jax.experimental.pallas import tpu as pltpu
from jax.sharding import PartitionSpec as P

F32 = jnp.float32
BF16 = jnp.bfloat16
VMEM_BYTES = 52 * 1024 * 1024


def dot(a, b, ca, cb):
    return lax.dot_general(a, b, (((ca,), (cb,)), ((), ())), preferred_element_type=F32)


def params():
    return pltpu.CompilerParams(vmem_limit_bytes=VMEM_BYTES)


def my_core():
    return lax.axis_index("hid") % 2


def chip_columns(k, width):
    chip = (lax.axis_index("hid") // 2) ^ k
    return pl.ds(pl.multiple_of(chip * (2 * width), 2 * width), 2 * width)


def call(kernel, name, operands, outs, scratch, flops, nbytes, alias=None, vmem=VMEM_BYTES):
    return pl.pallas_call(
        kernel,
        in_specs=[pl.BlockSpec(memory_space=pl.ANY)] * len(operands),
        out_specs=[pl.BlockSpec(memory_space=pl.ANY)] * len(outs),
        out_shape=[jax.ShapeDtypeStruct(shape, kind) for shape, kind in outs],
        scratch_shapes=scratch,
        input_output_aliases={} if alias is None else {alias: 0},
        compiler_params=pltpu.CompilerParams(vmem_limit_bytes=vmem),
        cost_estimate=pl.CostEstimate(flops=flops, bytes_accessed=nbytes, transcendentals=0),
        name=name,
    )(*operands)


def copies(sems, *pairs):
    made = [pltpu.make_async_copy(src, dst, sems.at[i]) for i, (src, dst) in enumerate(pairs)]
    for c in made:
        c.start()
    return made


def wait_all(made):
    for c in made:
        c.wait()


def dma(count):
    return pltpu.SemaphoreType.DMA((count,))


def start_each(steps, make):
    def one(j, carry):
        make(j).start()
        return carry

    lax.fori_loop(0, steps, one, 0)


def wait_each(steps, make):
    def one(j, carry):
        make(j).wait()
        return carry

    lax.fori_loop(0, steps, one, 0)


def each(steps, body):
    def one(j, carry):
        body(j)
        return carry

    lax.fori_loop(0, steps, one, 0)


def stream(steps, ahead, make, body):
    for j in range(min(ahead, steps)):
        make(j).start()

    def one(j):
        make(j).wait()

        @pl.when(j + ahead < steps)
        def _():
            make(j + ahead).start()

        body(j)

    each(steps, one)


def order_kernel(
    mask_ref, tokens_ref, upstream_ref, one_hot_ref, tokens_out, grad_out, mask_v, tokens_v, upstream_v, one_hot_v, out_v, grad_v, sems
):
    made = copies(sems, (mask_ref, mask_v), (tokens_ref, tokens_v), (upstream_ref, upstream_v))
    tok = tokens_v.shape[0]
    live = tok // 2
    made[0].wait()
    mask = mask_v[...].astype(F32)
    before = lax.broadcasted_iota(jnp.int32, (tok, tok), 0) < lax.broadcasted_iota(jnp.int32, (tok, tok), 1)
    rank = dot(jnp.broadcast_to(mask, (8, tok)).astype(BF16), before.astype(F32).astype(BF16), 1, 0)[:1]
    column = lax.broadcasted_iota(jnp.int32, (1, tok), 1).astype(F32)
    place = jnp.where(mask > 0, rank, live + column - rank)
    row = lax.broadcasted_iota(jnp.int32, (tok, tok), 0).astype(F32)
    one_hot = (row == place).astype(F32).astype(BF16)
    one_hot_v[...] = one_hot
    made[1].wait()
    out_v[...] = dot(tokens_v[...], one_hot, 0, 1).astype(BF16)
    made[2].wait()
    out = copies(sems, (one_hot_v, one_hot_ref), (out_v, tokens_out))
    grad_v[...] = dot(upstream_v[...], one_hot[:live], 0, 1).astype(BF16)
    wait_all(out + copies(sems.at[pl.ds(2, 1)], (grad_v, grad_out)))


def order_tokens(tokens, upstream, loss_mask):
    tok, width = tokens.shape
    outs = [((tok, tok), BF16), ((width, tok), BF16), ((width, tok // 2), BF16)]
    return call(
        order_kernel,
        "order_tokens",
        (loss_mask.reshape(1, tok), tokens, upstream),
        outs,
        [
            pltpu.VMEM((1, tok), jnp.int32),
            pltpu.VMEM((tok, width), BF16),
            pltpu.VMEM((tok, width), BF16),
            *[pltpu.VMEM(*out) for out in outs],
            dma(3),
        ],
        3 * tok * tok * width,
        8 * tok * width,
        vmem=62 * 1024 * 1024,
    )


def row_columns(k, wide):
    row = (lax.axis_index("hid") // 4) ^ k
    return pl.ds(pl.multiple_of(row * wide, wide), wide)


def row_copies(mine, other, dst):
    rows, wide, _ = dst.shape
    width = wide // 4
    in_row = lax.axis_index("hid") % 4
    pairs = []
    for chip in range(2 * rows):
        for flipped, part in enumerate((mine, other)):
            at = pl.ds(pl.multiple_of((in_row ^ (2 * (chip % 2) + flipped)) * width, width), width)
            pairs.append((part[chip], dst.at[chip // 2, at]))
    return pairs


def with_last(most, last):
    return [most.at[k] for k in range(most.shape[0])] + [last.at[0]]


def even_odd(even, odd):
    return [(even, odd)[k % 2].at[k // 2] for k in range(2 * even.shape[0])]


def piece_copies(sems, total, rounded, keep_ref, send_ref):
    rows, _, wide = total.shape
    width = wide // 4
    in_row = lax.axis_index("hid") % 4
    pairs = []
    for row in range(rows):
        for side in range(2):
            at = [pl.ds(pl.multiple_of((in_row ^ (2 * side + i)) * width, width), width) for i in range(2)]
            pairs.append((total.at[row, :, at[0]], keep_ref.at[2 * row + side]))
            pairs.append((rounded.at[row, :, at[1]], send_ref.at[2 * row + side]))
    return copies(sems, *pairs)


def start_gate_up(gate_w, up_w, base, j, buffer, sem):
    wide = buffer.shape[1]
    for i, weight in enumerate((gate_w, up_w)):

        @pl.when(j % 2 == i)
        def _():
            pltpu.make_async_copy(weight.at[:, row_columns(base + j // 2, wide)], buffer, sem).start()


def start_down(down_w, j, buffer, sem):
    pltpu.make_async_copy(down_w.at[:, row_columns(j, buffer.shape[1])], buffer, sem).start()


def wait_block(down_w, buffer, sem):
    pltpu.make_async_copy(down_w.at[:, pl.ds(0, buffer.shape[1])], buffer, sem).wait()


def forward_kernel(
    mine, mine_last, other, other_last, gate_w, up_w, down_w, x_ref, hidden_t_ref, act_ref, slope_ref, *rest
):
    keep_even, keep_odd, send_even, send_odd = rest[:4]
    x, w, acc, hidden_v, hidden_t_v, act_v, slope_v, total, rounded, sems, x_sems, w_sems, out_sems = rest[4:]
    slots = w.shape[0]
    rows = x.shape[0]
    steps = 2 * rows

    def start(j):
        slot = j % slots
        start_gate_up(gate_w, up_w, 0, j, w.at[slot], w_sems.at[slot])

    def start_last(j):
        start_down(down_w, j, w.at[j % slots], w_sems.at[j % slots])

    x_pairs = row_copies(with_last(mine, mine_last), with_last(other, other_last), x)
    x_in = copies(x_sems, *x_pairs[:4])
    start(0)
    x_in += copies(x_sems.at[pl.ds(4, 4 * rows - 4)], *x_pairs[4:])
    start(1)
    acc[...] = jnp.zeros_like(acc)

    def one(j):
        slot = j % slots
        for row in range(rows):

            @pl.when(j == 2 * row)
            def _():
                wait_all(x_in[4 * row : 4 * row + 4])

        wait_block(gate_w, w.at[slot], w_sems.at[slot])

        @pl.when(j + 2 < steps)
        def _():
            start(j + 2)

        @pl.when(j + 2 >= steps)
        def _():
            start_last(j + 2 - steps)

        acc[j % 2] += dot(w[slot], x[j // 2], 1, 0)

    each(steps, one)
    live = act_v.shape[1]
    out = copies(sems, (x.at[:, :, pl.ds(0, live)], x_ref))
    gate_lin = acc[0]
    up_lin = acc[1]
    sig = jax.nn.sigmoid(gate_lin)
    act = gate_lin * sig
    hidden = (act * up_lin).astype(BF16)
    hidden_t_v[...] = hidden[:, :live]
    act_v[...] = act[:, :live]
    slope_v[...] = (up_lin * sig * (1.0 + gate_lin * (1.0 - sig)))[:, :live]
    hidden_v[...] = hidden.T
    out += copies(sems.at[pl.ds(1, 3)], (hidden_t_v, hidden_t_ref), (act_v, act_ref), (slope_v, slope_ref))

    wide = x.shape[1]
    width = wide // 4
    in_row = lax.axis_index("hid") % 4
    at = [pl.ds(pl.multiple_of((in_row ^ i) * width, width), width) for i in range(4)]

    def out_copies(j):
        pairs = (
            (rounded.at[j, :, at[3]], send_odd.at[j]),
            (rounded.at[j, :, at[2]], keep_odd.at[j]),
            (rounded.at[j, :, at[1]], send_even.at[j]),
            (total.at[j, :, at[0]], keep_even.at[j]),
        )
        return [pltpu.make_async_copy(src, dst, out_sems.at[4 * j + i]) for i, (src, dst) in enumerate(pairs)]

    def two(j):
        slot = j % slots
        wait_block(down_w, w.at[slot], w_sems.at[slot])

        @pl.when(j + 2 < rows)
        def _():
            start_last(j + 2)

        part = dot(hidden_v[...], w[slot], 1, 0)
        total[j] = part
        rounded[j] = part.astype(BF16)
        for c in out_copies(j):
            c.start()

    each(rows, two)
    for j in range(rows):
        wait_all(out_copies(j))
    wait_all(out)


def forward(mine, other, gate_w, up_w, down_w, live):
    _, width, tok = mine[0].shape
    ff, features = gate_w.shape
    chips = features // (2 * width)
    rows, slots = chips // 2, 4
    return call(
        forward_kernel,
        "forward",
        (*mine, *other, gate_w, up_w, down_w),
        [
            ((rows, 4 * width, live), BF16),
            ((ff, live), BF16),
            ((ff, live), F32),
            ((ff, live), F32),
            ((rows, tok, width), F32),
            ((rows, tok, width), BF16),
            ((rows, tok, width), BF16),
            ((rows, tok, width), BF16),
        ],
        [
            pltpu.VMEM((rows, 4 * width, tok), BF16),
            pltpu.VMEM((slots, ff, 4 * width), BF16),
            pltpu.VMEM((2, ff, tok), F32),
            pltpu.VMEM((tok, ff), BF16),
            pltpu.VMEM((ff, live), BF16),
            pltpu.VMEM((ff, live), F32),
            pltpu.VMEM((ff, live), F32),
            pltpu.VMEM((rows, tok, 4 * width), F32),
            pltpu.VMEM((rows, tok, 4 * width), BF16),
            dma(4),
            dma(2 * chips),
            dma(slots),
            dma(4 * rows),
        ],
        12 * chips * width * ff * tok,
        12 * chips * width * ff,
    )


def backward_kernel(
    mine, mine_odd, other, other_odd, act_ref, slope_ref, gate_w, up_w, down_w, g_ref, d_gate_ref, d_up_ref, *rest
):
    keep_ref, send_ref, g, act, slope, w, acc, *rest = rest
    d_hid, d_hid_t, total, rounded, sems, g_sems, w_sems, out_sems = rest
    slots = w.shape[0]
    rows = g.shape[0]
    steps = 2 * rows

    def start_first(j):
        start_down(down_w, j, w.at[j % slots], w_sems.at[j % slots])

    def start(j):
        slot = j % slots
        start_gate_up(gate_w, up_w, 0, j, w.at[slot], w_sems.at[slot])

    first = copies(g_sems, *row_copies(even_odd(mine, mine_odd), even_odd(other, other_odd), g))
    start_first(0)
    start_first(1)
    late = copies(sems, (act_ref, act), (slope_ref, slope))
    acc[...] = jnp.zeros_like(acc)
    total[...] = jnp.zeros_like(total)
    wait_all(first)

    def one(j):
        slot = j % slots
        wait_block(down_w, w.at[slot], w_sems.at[slot])

        @pl.when(j + 2 < rows)
        def _():
            start_first(j + 2)

        @pl.when(j + 2 >= rows)
        def _():
            start(j + 2 - rows)

        acc[...] += dot(w[slot], g[j], 1, 0)

    each(rows, one)
    wait_all(late)
    d_gate = (acc[...] * slope[...]).astype(BF16)
    d_up = (acc[...] * act[...]).astype(BF16)
    d_hid_t[0] = d_gate
    d_hid_t[1] = d_up
    d_hid[0] = d_gate.T
    d_hid[1] = d_up.T
    out = copies(sems, (d_hid_t.at[0], d_gate_ref), (d_hid_t.at[1], d_up_ref), (g, g_ref))

    def two(j):
        slot = j % slots
        wait_block(gate_w, w.at[slot], w_sems.at[slot])

        @pl.when(j + 2 < steps)
        def _():
            start(j + 2)

        part = total[j // 2] + dot(d_hid[j % 2], w[slot], 1, 0)
        total[j // 2] = part
        rounded[j // 2] = part.astype(BF16)

    each(steps, two)
    wait_all(out + piece_copies(out_sems, total, rounded, keep_ref, send_ref))


def backward(mine, other, act, slope, gate_w, up_w, down_w):
    _, width, live = mine[0].shape
    ff = act.shape[0]
    chips = down_w.shape[1] // (2 * width)
    rows, slots = chips // 2, 4
    d_hid_t = ((ff, live), BF16)
    return call(
        backward_kernel,
        "backward",
        (*mine, *other, act, slope, gate_w, up_w, down_w),
        [((rows, 4 * width, live), BF16), d_hid_t, d_hid_t, ((chips, live, width), F32), ((chips, live, width), BF16)],
        [
            pltpu.VMEM((rows, 4 * width, live), BF16),
            pltpu.VMEM((ff, live), F32),
            pltpu.VMEM((ff, live), F32),
            pltpu.VMEM((slots, ff, 4 * width), BF16),
            pltpu.VMEM((ff, live), F32),
            pltpu.VMEM((2, live, ff), BF16),
            pltpu.VMEM((2, ff, live), BF16),
            pltpu.VMEM((rows, live, 4 * width), F32),
            pltpu.VMEM((rows, live, 4 * width), BF16),
            dma(3),
            dma(2 * chips),
            dma(slots),
            dma(2 * chips),
        ],
        6 * live * down_w.size,
        6 * down_w.size,
    )


def weight_grad_kernel(base, hid_ref, x_ref, *refs):
    out_ref, hid, x, out_v, sems, out_sems = refs[-6:]
    steps = out_v.shape[0]
    rows, wide, _ = x.shape
    half = wide // 2
    ready = copies(sems, (hid_ref, hid), *[(x_ref.at[base + row], x.at[row]) for row in range(rows)])

    def out_copy(j):
        row = (lax.axis_index("hid") // 4) ^ (base + j // 2)
        at = pl.ds(pl.multiple_of(row * wide + (j % 2) * half, half), half)
        return pltpu.make_async_copy(out_v.at[j], out_ref.at[:, at], out_sems.at[j])

    ready[0].wait()

    def step(j):
        for row in range(rows):

            @pl.when(j == 2 * row)
            def _():
                ready[1 + row].wait()

        out_v[j] = dot(hid[...], x[j // 2, pl.ds(pl.multiple_of((j % 2) * half, half), half), :], 1, 1).astype(BF16)
        out_copy(j).start()

    each(steps, step)
    wait_each(steps, out_copy)


def weight_grad(hid, x, name, base=0, rows=4, before=None):
    all_rows, wide, live = x.shape
    ff = hid.shape[-2]
    steps = 2 * rows
    return call(
        functools.partial(weight_grad_kernel, base),
        name,
        (hid, x) if before is None else (hid, x, before),
        [((ff, all_rows * wide), BF16)],
        [
            pltpu.VMEM((ff, live), BF16),
            pltpu.VMEM((rows, wide, live), BF16),
            pltpu.VMEM((steps, ff, wide // 2), BF16),
            dma(1 + rows),
            dma(steps),
        ],
        2 * live * ff * rows * wide,
        2 * ff * rows * wide,
        None if before is None else 2,
        24 * 1024 * 1024,
    )[0]


def last_kernel(one_hot, *refs):
    total = refs[0][...].astype(F32)
    for part in refs[1:-1]:
        total = total + part[...].astype(F32)
    refs[-1][...] = dot(one_hot[...], total.astype(BF16), 0, 0).astype(BF16)


def last_sum(one_hot, parts, name):
    return pl.pallas_call(
        last_kernel,
        out_shape=jax.ShapeDtypeStruct((one_hot.shape[1], parts[0].shape[1]), BF16),
        compiler_params=params(),
        name=name,
    )(one_hot, *parts)


def flip(x, bits):
    return lax.ppermute(x, "hid", [(i, i ^ bits) for i in range(16)])


def plus(a, b):
    return a.astype(F32) + b.astype(F32)


def join(*arrays):
    return lax.optimization_barrier(arrays)


def body16(tokens, upstream, loss_mask, gate_weight, up_weight, down_weight):
    tok, width = tokens.shape
    live = tok // 2
    gate_w, up_w = gate_weight.T, up_weight.T
    one_hot, x, g = order_tokens(tokens, upstream, loss_mask)
    z2, z1, y, gz1 = flip(x, 8), flip(x, 4), flip(x, 2), flip(g, 4)
    gz1, y, z1, z2, g = join(gz1, y, z1, z2, g)
    z3, yz1, yz2, gz2 = flip(z2, 4), flip(z1, 2), flip(z2, 2), flip(g, 8)
    gz2, yz2, yz1, z3, g = join(gz2, yz2, yz1, z3, g)
    yz3 = flip(z3, 2)
    most = jnp.stack([x, y, z1, yz1, z2, yz2, z3])
    most_other = flip(most, 1)
    gz3 = flip(g, 12)
    gz3, most_other, yz3 = join(gz3, most_other, yz3)
    g_even = jnp.stack([g, gz1, gz2, gz3])
    g_odd, g_even_other = flip(g_even, 2), flip(g_even, 1)
    x_mine, x_other = (most, yz3[None]), (most_other, flip(yz3, 1)[None])
    x_rows, hidden_t, act, slope, keep_even, keep_odd, send_even, send_odd = forward(
        x_mine, x_other, gate_w, up_w, down_weight, live
    )
    send_odd, g_odd, g_even_other = join(send_odd, g_odd, g_even_other)
    recv_odd, g_odd_other = flip(send_odd, 1), flip(g_odd, 1)
    recv_odd, g_odd_other, send_even = join(recv_odd, g_odd_other, send_even)
    recv_even = flip(send_even, 1)
    out_y = flip(plus(keep_odd, recv_odd).astype(BF16), 2)
    g_rows, d_gate_t, d_up_t, tk, ts = backward(
        (g_even, g_odd), (g_even_other, g_odd_other), act, slope, gate_w, up_w, down_weight
    )
    ts, out_y, recv_even, hidden_t = join(ts, out_y, recv_even, hidden_t)
    rows = [plus(keep_even[k], recv_even[k]) + out_y[k].astype(F32) for k in range(4)]
    t_recv = flip(ts, 1)
    z13 = flip(rows[3].astype(BF16), 4)
    down_grad = weight_grad(hidden_t, g_rows, "down_grad")
    down_grad, z13, t_recv, d_gate_t = join(down_grad, z13, t_recv, d_gate_t)
    z2 = flip((rows[2] + z13.astype(F32)).astype(BF16), 8)
    z1 = flip(rows[1].astype(BF16), 4)
    t_y23 = flip(plus(tk[5::2], t_recv[5::2]).astype(BF16), 2)
    gate_grad = weight_grad(d_gate_t, x_rows, "gate_grad")
    gate_grad, d_up_t, t_y23, t_recv = join(gate_grad, d_up_t, t_y23, t_recv)
    tz13 = flip((plus(tk[6], t_recv[6]) + t_y23[1].astype(F32)).astype(BF16), 4)
    t_y01 = flip(plus(tk[1:4:2], t_recv[1:4:2]).astype(BF16), 2)
    up_grad = weight_grad(d_up_t, x_rows, "up_grad_0", 0, 2)
    up_grad, tz13, t_y01, z2, z1 = join(up_grad, tz13, t_y01, z2, z1)
    tz2 = flip((plus(tk[4], t_recv[4]) + plus(t_y23[0], tz13)).astype(BF16), 8)
    tz1 = flip((plus(tk[2], t_recv[2]) + t_y01[1].astype(F32)).astype(BF16), 4)
    ffn_output = last_sum(one_hot, (rows[0], z2, z1), "ffn_output")
    up_grad = weight_grad(d_up_t, x_rows, "up_grad_1", 2, 2, up_grad)
    up_grad, tz2, tz1 = join(up_grad, tz2, tz1)
    token_grad = last_sum(one_hot[:live], (plus(tk[0], t_recv[0]) + t_y01[0].astype(F32), tz2, tz1), "token_grad")
    return ffn_output, token_grad, gate_grad.T, up_grad.T, down_grad


def body_any(tokens, upstream, loss_mask, gate_weight, up_weight, down_weight):
    masked = upstream * loss_mask[:, None].astype(upstream.dtype)
    tokens = lax.all_gather(tokens, "hid", axis=1, tiled=True)
    grad = lax.all_gather(masked, "hid", axis=1, tiled=True)
    gate_lin = dot(tokens, gate_weight, 1, 0)
    up_lin = dot(tokens, up_weight, 1, 0)
    sig = jax.nn.sigmoid(gate_lin)
    act = gate_lin * sig
    hidden = (act * up_lin).astype(BF16)
    out = lax.psum_scatter(dot(down_weight, hidden, 0, 1), "hid", scatter_dimension=0, tiled=True)
    d_hidden = dot(grad, down_weight, 1, 1)
    d_up = (d_hidden * act).astype(BF16)
    d_gate = (d_hidden * up_lin * sig * (1.0 + gate_lin * (1.0 - sig))).astype(BF16)
    down_grad = dot(hidden, grad, 0, 0).astype(BF16)
    gate_grad = dot(tokens, d_gate, 0, 0).astype(BF16)
    up_grad = dot(tokens, d_up, 0, 0).astype(BF16)
    back = dot(gate_weight, d_gate, 1, 1) + dot(up_weight, d_up, 1, 1)
    back = lax.psum_scatter(back, "hid", scatter_dimension=0, tiled=True)
    return out.T.astype(BF16), back.T.astype(BF16), gate_grad, up_grad, down_grad


def solution(mesh):
    spec = P("groups", "hid")
    in_specs = (spec, spec, P("groups"), P(None, "hid"), P(None, "hid"), P("hid", None))
    out_specs = (spec, spec, spec, spec, P("hid", "groups"))
    body = body16 if mesh.shape["hid"] == 16 else body_any
    return jax.shard_map(body, mesh=mesh, in_specs=in_specs, out_specs=out_specs, check_vma=False)
```

```python
import functools

import jax
import jax.numpy as jnp
from jax import lax
from jax.experimental import pallas as pl
from jax.experimental.pallas import tpu as pltpu
from jax.sharding import PartitionSpec as P

F32 = jnp.float32
BF16 = jnp.bfloat16
VMEM_BYTES = 52 * 1024 * 1024


def dot(a, b, ca, cb):
    return lax.dot_general(a, b, (((ca,), (cb,)), ((), ())), preferred_element_type=F32)


def params():
    return pltpu.CompilerParams(vmem_limit_bytes=VMEM_BYTES)


def my_core():
    return lax.axis_index("hid") % 2


def chip_columns(k, width):
    chip = (lax.axis_index("hid") // 2) ^ k
    return pl.ds(pl.multiple_of(chip * (2 * width), 2 * width), 2 * width)


def call(kernel, name, operands, outs, scratch, flops, nbytes, vmem=VMEM_BYTES):
    return pl.pallas_call(
        kernel,
        in_specs=[pl.BlockSpec(memory_space=pl.ANY)] * len(operands),
        out_specs=[pl.BlockSpec(memory_space=pl.ANY)] * len(outs),
        out_shape=[jax.ShapeDtypeStruct(shape, kind) for shape, kind in outs],
        scratch_shapes=scratch,
        compiler_params=pltpu.CompilerParams(vmem_limit_bytes=vmem),
        cost_estimate=pl.CostEstimate(flops=flops, bytes_accessed=nbytes, transcendentals=0),
        name=name,
    )(*operands)


def copies(sems, *pairs):
    made = [pltpu.make_async_copy(src, dst, sems.at[i]) for i, (src, dst) in enumerate(pairs)]
    for c in made:
        c.start()
    return made


def wait_all(made):
    for c in made:
        c.wait()


def dma(count):
    return pltpu.SemaphoreType.DMA((count,))


def start_each(steps, make):
    def one(j, carry):
        make(j).start()
        return carry

    lax.fori_loop(0, steps, one, 0)


def wait_each(steps, make):
    def one(j, carry):
        make(j).wait()
        return carry

    lax.fori_loop(0, steps, one, 0)


def each(steps, body):
    def one(j, carry):
        body(j)
        return carry

    lax.fori_loop(0, steps, one, 0)


def stream(steps, ahead, make, body):
    for j in range(min(ahead, steps)):
        make(j).start()

    def one(j):
        make(j).wait()

        @pl.when(j + ahead < steps)
        def _():
            make(j + ahead).start()

        body(j)

    each(steps, one)


def order_kernel(
    mask_ref, tokens_ref, upstream_ref, one_hot_ref, tokens_out, grad_out, mask_v, tokens_v, upstream_v, one_hot_v, out_v, grad_v, sems
):
    made = copies(sems, (mask_ref, mask_v), (tokens_ref, tokens_v), (upstream_ref, upstream_v))
    tok = tokens_v.shape[0]
    live = tok // 2
    made[0].wait()
    mask = mask_v[...].astype(F32)
    before = lax.broadcasted_iota(jnp.int32, (tok, tok), 0) < lax.broadcasted_iota(jnp.int32, (tok, tok), 1)
    rank = dot(jnp.broadcast_to(mask, (8, tok)).astype(BF16), before.astype(F32).astype(BF16), 1, 0)[:1]
    column = lax.broadcasted_iota(jnp.int32, (1, tok), 1).astype(F32)
    place = jnp.where(mask > 0, rank, live + column - rank)
    row = lax.broadcasted_iota(jnp.int32, (tok, tok), 0).astype(F32)
    one_hot = (row == place).astype(F32).astype(BF16)
    one_hot_v[...] = one_hot
    made[1].wait()
    out_v[...] = dot(tokens_v[...], one_hot, 0, 1).astype(BF16)
    made[2].wait()
    out = copies(sems, (one_hot_v, one_hot_ref), (out_v, tokens_out))
    grad_v[...] = dot(upstream_v[...], one_hot[:live], 0, 1).astype(BF16)
    wait_all(out + copies(sems.at[pl.ds(2, 1)], (grad_v, grad_out)))


def order_tokens(tokens, upstream, loss_mask):
    tok, width = tokens.shape
    outs = [((tok, tok), BF16), ((width, tok), BF16), ((width, tok // 2), BF16)]
    return call(
        order_kernel,
        "order_tokens",
        (loss_mask.reshape(1, tok), tokens, upstream),
        outs,
        [
            pltpu.VMEM((1, tok), jnp.int32),
            pltpu.VMEM((tok, width), BF16),
            pltpu.VMEM((tok, width), BF16),
            *[pltpu.VMEM(*out) for out in outs],
            dma(3),
        ],
        3 * tok * tok * width,
        8 * tok * width,
        vmem=62 * 1024 * 1024,
    )


def row_columns(k, wide):
    row = (lax.axis_index("hid") // 4) ^ k
    return pl.ds(pl.multiple_of(row * wide, wide), wide)


def row_copies(mine, other, dst):
    rows, wide, _ = dst.shape
    width = wide // 4
    in_row = lax.axis_index("hid") % 4
    pairs = []
    for chip in range(2 * rows):
        for flipped, part in enumerate((mine, other)):
            at = pl.ds(pl.multiple_of((in_row ^ (2 * (chip % 2) + flipped)) * width, width), width)
            pairs.append((part[chip], dst.at[chip // 2, at]))
    return pairs


def with_last(most, last):
    return [most.at[k] for k in range(most.shape[0])] + [last.at[0]]


def even_odd(even, odd):
    return [(even, odd)[k % 2].at[k // 2] for k in range(2 * even.shape[0])]


def part_copies(j, total, rounded, outs, sems):
    width = total.shape[2] // 4
    in_row = lax.axis_index("hid") % 4
    keep_even, keep_odd, send_even, send_odd = outs
    made = []
    for i, (src, dst) in enumerate(((total, keep_even), (rounded, send_even), (rounded, keep_odd), (rounded, send_odd))):
        at = pl.ds(pl.multiple_of((in_row ^ i) * width, width), width)
        made.append(pltpu.make_async_copy(src.at[j, :, at], dst.at[j], sems.at[4 * j + i]))
    return made


def part_outs(rows, tok, width):
    return [((rows, tok, width), F32)] + 3 * [((rows, tok, width), BF16)]


def start_gate_up(gate_w, up_w, base, j, buffer, sem):
    wide = buffer.shape[1]
    for i, weight in enumerate((gate_w, up_w)):

        @pl.when(j % 2 == i)
        def _():
            pltpu.make_async_copy(weight.at[:, row_columns(base + j // 2, wide)], buffer, sem).start()


def start_down(down_w, j, buffer, sem):
    pltpu.make_async_copy(down_w.at[:, row_columns(j, buffer.shape[1])], buffer, sem).start()


def wait_block(down_w, buffer, sem):
    pltpu.make_async_copy(down_w.at[:, pl.ds(0, buffer.shape[1])], buffer, sem).wait()


def forward_kernel(
    mine, mine_last, other, other_last, gate_w, up_w, down_w, x_ref, hidden_t_ref, act_ref, slope_ref, *rest
):
    parts = rest[:4]
    x, w, acc, hidden_v, hidden_t_v, act_v, slope_v, total, rounded, sems, x_sems, w_sems, out_sems = rest[4:]
    slots = w.shape[0]
    rows = x.shape[0]
    steps = 2 * rows

    def start(j):
        slot = j % slots
        start_gate_up(gate_w, up_w, 0, j, w.at[slot], w_sems.at[slot])

    def start_last(j):
        start_down(down_w, j, w.at[j % slots], w_sems.at[j % slots])

    x_pairs = row_copies(with_last(mine, mine_last), with_last(other, other_last), x)
    x_in = copies(x_sems, *x_pairs[:4])
    start(0)
    x_in += copies(x_sems.at[pl.ds(4, 4 * rows - 4)], *x_pairs[4:])
    start(1)
    acc[...] = jnp.zeros_like(acc)

    def one(j):
        slot = j % slots
        for row in range(rows):

            @pl.when(j == 2 * row)
            def _():
                wait_all(x_in[4 * row : 4 * row + 4])

        wait_block(gate_w, w.at[slot], w_sems.at[slot])

        @pl.when(j + 2 < steps)
        def _():
            start(j + 2)

        @pl.when(j + 2 >= steps)
        def _():
            start_last(j + 2 - steps)

        acc[j % 2] += dot(w[slot], x[j // 2], 1, 0)

    each(steps, one)
    live = act_v.shape[1]
    out = copies(sems, (x.at[:, :, pl.ds(0, live)], x_ref))
    gate_lin = acc[0]
    up_lin = acc[1]
    sig = jax.nn.sigmoid(gate_lin)
    act = gate_lin * sig
    hidden = (act * up_lin).astype(BF16)
    hidden_t_v[...] = hidden[:, :live]
    act_v[...] = act[:, :live]
    slope_v[...] = (up_lin * sig * (1.0 + gate_lin * (1.0 - sig)))[:, :live]
    hidden_v[...] = hidden.T
    out += copies(sems.at[pl.ds(1, 3)], (hidden_t_v, hidden_t_ref), (act_v, act_ref), (slope_v, slope_ref))

    def two(j):
        slot = j % slots
        wait_block(down_w, w.at[slot], w_sems.at[slot])

        @pl.when(j + 2 < rows)
        def _():
            start_last(j + 2)

        part = dot(hidden_v[...], w[slot], 1, 0)
        total[j] = part
        rounded[j] = part.astype(BF16)
        for c in part_copies(j, total, rounded, parts, out_sems):
            c.start()

    each(rows, two)
    for j in range(rows):
        wait_all(part_copies(j, total, rounded, parts, out_sems))
    wait_all(out)


def forward(mine, other, gate_w, up_w, down_w, live):
    _, width, tok = mine[0].shape
    ff, features = gate_w.shape
    chips = features // (2 * width)
    rows, slots = chips // 2, 4
    return call(
        forward_kernel,
        "forward",
        (*mine, *other, gate_w, up_w, down_w),
        [
            ((rows, 4 * width, live), BF16),
            ((ff, live), BF16),
            ((ff, live), F32),
            ((ff, live), F32),
            *part_outs(rows, tok, width),
        ],
        [
            pltpu.VMEM((rows, 4 * width, tok), BF16),
            pltpu.VMEM((slots, ff, 4 * width), BF16),
            pltpu.VMEM((2, ff, tok), F32),
            pltpu.VMEM((tok, ff), BF16),
            pltpu.VMEM((ff, live), BF16),
            pltpu.VMEM((ff, live), F32),
            pltpu.VMEM((ff, live), F32),
            pltpu.VMEM((rows, tok, 4 * width), F32),
            pltpu.VMEM((rows, tok, 4 * width), BF16),
            dma(4),
            dma(2 * chips),
            dma(slots),
            dma(4 * rows),
        ],
        12 * chips * width * ff * tok,
        12 * chips * width * ff,
        vmem=48 * 1024 * 1024,
    )


def backward_kernel(
    mine, mine_odd, other, other_odd, act_ref, slope_ref, gate_w, up_w, down_w, g_ref, d_gate_ref, d_up_ref, *rest
):
    parts = rest[:4]
    g, act, slope, w, acc, *rest = rest[4:]
    d_hid, d_hid_t, total, rounded, sems, g_sems, w_sems, out_sems = rest
    slots = w.shape[0]
    rows = g.shape[0]
    steps = 2 * rows

    def start_first(j):
        start_down(down_w, j, w.at[j % slots], w_sems.at[j % slots])

    def start(j):
        slot = j % slots
        start_gate_up(gate_w, up_w, 0, j, w.at[slot], w_sems.at[slot])

    first = copies(g_sems, *row_copies(even_odd(mine, mine_odd), even_odd(other, other_odd), g))
    start_first(0)
    start_first(1)
    late = copies(sems, (act_ref, act), (slope_ref, slope))
    acc[...] = jnp.zeros_like(acc)
    total[...] = jnp.zeros_like(total)
    wait_all(first)

    def one(j):
        slot = j % slots
        wait_block(down_w, w.at[slot], w_sems.at[slot])

        @pl.when(j + 2 < rows)
        def _():
            start_first(j + 2)

        @pl.when(j + 2 >= rows)
        def _():
            start(j + 2 - rows)

        acc[...] += dot(w[slot], g[j], 1, 0)

    each(rows, one)
    wait_all(late)
    d_gate = (acc[...] * slope[...]).astype(BF16)
    d_up = (acc[...] * act[...]).astype(BF16)
    d_hid_t[0] = d_gate
    d_hid_t[1] = d_up
    d_hid[0] = d_gate.T
    d_hid[1] = d_up.T
    out = copies(sems, (d_hid_t.at[0], d_gate_ref), (d_hid_t.at[1], d_up_ref), (g, g_ref))

    def two(j):
        slot = j % slots
        wait_block(gate_w, w.at[slot], w_sems.at[slot])

        @pl.when(j + 2 < steps)
        def _():
            start(j + 2)

        part = total[j // 2] + dot(d_hid[j % 2], w[slot], 1, 0)
        total[j // 2] = part
        rounded[j // 2] = part.astype(BF16)

        @pl.when(j % 2 == 1)
        def _():
            for c in part_copies(j // 2, total, rounded, parts, out_sems):
                c.start()

    each(steps, two)
    for j in range(rows):
        wait_all(part_copies(j, total, rounded, parts, out_sems))
    wait_all(out)


def backward(mine, other, act, slope, gate_w, up_w, down_w):
    _, width, live = mine[0].shape
    ff = act.shape[0]
    chips = down_w.shape[1] // (2 * width)
    rows, slots = chips // 2, 4
    d_hid_t = ((ff, live), BF16)
    return call(
        backward_kernel,
        "backward",
        (*mine, *other, act, slope, gate_w, up_w, down_w),
        [((rows, 4 * width, live), BF16), d_hid_t, d_hid_t, *part_outs(rows, live, width)],
        [
            pltpu.VMEM((rows, 4 * width, live), BF16),
            pltpu.VMEM((ff, live), F32),
            pltpu.VMEM((ff, live), F32),
            pltpu.VMEM((slots, ff, 4 * width), BF16),
            pltpu.VMEM((ff, live), F32),
            pltpu.VMEM((2, live, ff), BF16),
            pltpu.VMEM((2, ff, live), BF16),
            pltpu.VMEM((rows, live, 4 * width), F32),
            pltpu.VMEM((rows, live, 4 * width), BF16),
            dma(3),
            dma(2 * chips),
            dma(slots),
            dma(2 * chips),
        ],
        6 * live * down_w.size,
        6 * down_w.size,
        vmem=32 * 1024 * 1024,
    )


def weight_grad_kernel(hid_ref, x_ref, out_ref, hid, x, out_v, sems, out_sems):
    steps = out_v.shape[0]
    rows, wide, _ = x.shape
    half = wide // 2
    ready = copies(sems, (hid_ref, hid), *[(x_ref.at[row], x.at[row]) for row in range(rows)])

    def out_copy(j):
        row = (lax.axis_index("hid") // 4) ^ (j // 2)
        at = pl.ds(pl.multiple_of(row * wide + (j % 2) * half, half), half)
        return pltpu.make_async_copy(out_v.at[j], out_ref.at[:, at], out_sems.at[j])

    ready[0].wait()

    def step(j):
        for row in range(rows):

            @pl.when(j == 2 * row)
            def _():
                ready[1 + row].wait()

        out_v[j] = dot(hid[...], x[j // 2, pl.ds(pl.multiple_of((j % 2) * half, half), half), :], 1, 1).astype(BF16)
        out_copy(j).start()

    each(steps, step)
    wait_each(steps, out_copy)


def weight_grad(hid, x, name):
    rows, wide, live = x.shape
    ff = hid.shape[-2]
    steps = 2 * rows
    return call(
        weight_grad_kernel,
        name,
        (hid, x),
        [((ff, rows * wide), BF16)],
        [
            pltpu.VMEM((ff, live), BF16),
            pltpu.VMEM((rows, wide, live), BF16),
            pltpu.VMEM((steps, ff, wide // 2), BF16),
            dma(1 + rows),
            dma(steps),
        ],
        2 * live * ff * rows * wide,
        2 * ff * rows * wide,
        vmem=24 * 1024 * 1024,
    )[0]


def last_kernel(count, *refs):
    one_hot = refs[0][...]
    for i, out in enumerate(refs[-2:]):
        parts = refs[1 + i * count : 1 + (i + 1) * count]
        total = parts[0][...].astype(F32)
        for part in parts[1:]:
            total = total + part[...].astype(F32)
        out[...] = dot(one_hot[: total.shape[0]], total.astype(BF16), 0, 0).astype(BF16)


def last_sums(one_hot, first, second):
    tok = one_hot.shape[1]
    out = jax.ShapeDtypeStruct((tok, first[0].shape[1]), BF16)
    return pl.pallas_call(
        functools.partial(last_kernel, len(first)),
        out_shape=[out, out],
        compiler_params=params(),
        name="last_sums",
    )(one_hot, *first, *second)


def flip(x, bits):
    return lax.ppermute(x, "hid", [(i, i ^ bits) for i in range(16)])


def plus(a, b):
    return a.astype(F32) + b.astype(F32)


def join(*arrays):
    return lax.optimization_barrier(arrays)


def body16(tokens, upstream, loss_mask, gate_weight, up_weight, down_weight):
    tok, width = tokens.shape
    live = tok // 2
    gate_w, up_w = gate_weight.T, up_weight.T
    one_hot, x, g = order_tokens(tokens, upstream, loss_mask)
    z2, z1, y = flip(x, 8), flip(x, 4), flip(x, 2)
    yz1 = flip(z1, 2)
    yz1, y, z1, z2, g = join(yz1, y, z1, z2, g)
    z3, yz2, gz2 = flip(z2, 4), flip(z2, 2), flip(g, 8)
    gz2, yz2, z3, g = join(gz2, yz2, z3, g)
    yz3 = flip(z3, 2)
    most = jnp.stack([x, y, z1, yz1, z2, yz2, z3])
    most_other = flip(most, 1)
    gz3, gz1 = flip(g, 12), flip(g, 4)
    gz1, gz3, most_other, yz3 = join(gz1, gz3, most_other, yz3)
    g_even = jnp.stack([g, gz1, gz2, gz3])
    g_odd, g_even_other = flip(g_even, 2), flip(g_even, 1)
    x_mine, x_other = (most, yz3[None]), (most_other, flip(yz3, 1)[None])
    x_rows, hidden_t, act, slope, keep_even, keep_odd, send_even, send_odd = forward(
        x_mine, x_other, gate_w, up_w, down_weight, live
    )
    send_odd, g_odd, g_even_other = join(send_odd, g_odd, g_even_other)
    recv_odd, g_odd_other = flip(send_odd, 1), flip(g_odd, 1)
    recv_odd, g_odd_other, send_even = join(recv_odd, g_odd_other, send_even)
    recv_even = flip(send_even, 1)
    out_y = flip(plus(keep_odd, recv_odd).astype(BF16), 2)
    g_rows, d_gate_t, d_up_t, t_keep_even, t_keep_odd, t_send_even, t_send_odd = backward(
        (g_even, g_odd), (g_even_other, g_odd_other), act, slope, gate_w, up_w, down_weight
    )
    t_send_odd, out_y, recv_even = join(t_send_odd, out_y, recv_even)
    t_recv_odd = flip(t_send_odd, 1)
    rows = [plus(keep_even[k], recv_even[k]) + out_y[k].astype(F32) for k in range(4)]
    z13 = flip(rows[3].astype(BF16), 4)
    t_recv_odd, t_send_even, hidden_t = join(t_recv_odd, t_send_even, hidden_t)
    t_recv_even = flip(t_send_even, 1)
    t_y23 = flip(plus(t_keep_odd[2:], t_recv_odd[2:]).astype(BF16), 2)
    down_grad = weight_grad(hidden_t, g_rows, "down_grad")
    down_grad, z13, t_y23, t_recv_odd, t_recv_even, d_gate_t = join(
        down_grad, z13, t_y23, t_recv_odd, t_recv_even, d_gate_t
    )
    t_even = plus(t_keep_even, t_recv_even)
    z2 = flip((rows[2] + z13.astype(F32)).astype(BF16), 8)
    z1 = flip(rows[1].astype(BF16), 4)
    t_y01 = flip(plus(t_keep_odd[:2], t_recv_odd[:2]).astype(BF16), 2)
    tz13 = flip((t_even[3] + t_y23[1].astype(F32)).astype(BF16), 4)
    gate_grad = weight_grad(d_gate_t, x_rows, "gate_grad")
    gate_grad, d_up_t, tz13, t_y01, z2, z1 = join(gate_grad, d_up_t, tz13, t_y01, z2, z1)
    tz1 = flip((t_even[1] + t_y01[1].astype(F32)).astype(BF16), 4)
    tz2 = flip((t_even[2] + plus(t_y23[0], tz13)).astype(BF16), 8)
    up_grad = weight_grad(d_up_t, x_rows, "up_grad")
    up_grad, tz2, tz1 = join(up_grad, tz2, tz1)
    t_row = t_even[0] + t_y01[0].astype(F32)
    ffn_output, token_grad = last_sums(one_hot, (rows[0], z2, z1), (t_row, tz2, tz1))
    return ffn_output, token_grad, gate_grad.T, up_grad.T, down_grad


def body_any(tokens, upstream, loss_mask, gate_weight, up_weight, down_weight):
    masked = upstream * loss_mask[:, None].astype(upstream.dtype)
    tokens = lax.all_gather(tokens, "hid", axis=1, tiled=True)
    grad = lax.all_gather(masked, "hid", axis=1, tiled=True)
    gate_lin = dot(tokens, gate_weight, 1, 0)
    up_lin = dot(tokens, up_weight, 1, 0)
    sig = jax.nn.sigmoid(gate_lin)
    act = gate_lin * sig
    hidden = (act * up_lin).astype(BF16)
    out = lax.psum_scatter(dot(down_weight, hidden, 0, 1), "hid", scatter_dimension=0, tiled=True)
    d_hidden = dot(grad, down_weight, 1, 1)
    d_up = (d_hidden * act).astype(BF16)
    d_gate = (d_hidden * up_lin * sig * (1.0 + gate_lin * (1.0 - sig))).astype(BF16)
    down_grad = dot(hidden, grad, 0, 0).astype(BF16)
    gate_grad = dot(tokens, d_gate, 0, 0).astype(BF16)
    up_grad = dot(tokens, d_up, 0, 0).astype(BF16)
    back = dot(gate_weight, d_gate, 1, 1) + dot(up_weight, d_up, 1, 1)
    back = lax.psum_scatter(back, "hid", scatter_dimension=0, tiled=True)
    return out.T.astype(BF16), back.T.astype(BF16), gate_grad, up_grad, down_grad


def solution(mesh):
    spec = P("groups", "hid")
    in_specs = (spec, spec, P("groups"), P(None, "hid"), P(None, "hid"), P("hid", None))
    out_specs = (spec, spec, spec, spec, P("hid", "groups"))
    body = body16 if mesh.shape["hid"] == 16 else body_any
    return jax.shard_map(body, mesh=mesh, in_specs=in_specs, out_specs=out_specs, check_vma=False)
```

```python
import functools

import jax
import jax.numpy as jnp
from jax import lax
from jax.experimental import pallas as pl
from jax.experimental.pallas import tpu as pltpu
from jax.sharding import PartitionSpec as P

F32 = jnp.float32
BF16 = jnp.bfloat16
VMEM_BYTES = 52 * 1024 * 1024


def dot(a, b, ca, cb):
    return lax.dot_general(a, b, (((ca,), (cb,)), ((), ())), preferred_element_type=F32)


def params():
    return pltpu.CompilerParams(vmem_limit_bytes=VMEM_BYTES)


def my_core():
    return lax.axis_index("hid") % 2


def chip_columns(k, width):
    chip = (lax.axis_index("hid") // 2) ^ k
    return pl.ds(pl.multiple_of(chip * (2 * width), 2 * width), 2 * width)


def call(kernel, name, operands, outs, scratch, flops, nbytes, vmem=VMEM_BYTES):
    return pl.pallas_call(
        kernel,
        in_specs=[pl.BlockSpec(memory_space=pl.ANY)] * len(operands),
        out_specs=[pl.BlockSpec(memory_space=pl.ANY)] * len(outs),
        out_shape=[jax.ShapeDtypeStruct(shape, kind) for shape, kind in outs],
        scratch_shapes=scratch,
        compiler_params=pltpu.CompilerParams(vmem_limit_bytes=vmem),
        cost_estimate=pl.CostEstimate(flops=flops, bytes_accessed=nbytes, transcendentals=0),
        name=name,
    )(*operands)


def copies(sems, *pairs):
    made = [pltpu.make_async_copy(src, dst, sems.at[i]) for i, (src, dst) in enumerate(pairs)]
    for c in made:
        c.start()
    return made


def wait_all(made):
    for c in made:
        c.wait()


def dma(count):
    return pltpu.SemaphoreType.DMA((count,))


def start_each(steps, make):
    def one(j, carry):
        make(j).start()
        return carry

    lax.fori_loop(0, steps, one, 0)


def wait_each(steps, make):
    def one(j, carry):
        make(j).wait()
        return carry

    lax.fori_loop(0, steps, one, 0)


def each(steps, body):
    def one(j, carry):
        body(j)
        return carry

    lax.fori_loop(0, steps, one, 0)


def stream(steps, ahead, make, body):
    for j in range(min(ahead, steps)):
        make(j).start()

    def one(j):
        make(j).wait()

        @pl.when(j + ahead < steps)
        def _():
            make(j + ahead).start()

        body(j)

    each(steps, one)


def order_kernel(
    mask_ref, tokens_ref, upstream_ref, one_hot_ref, tokens_out, grad_out, mask_v, tokens_v, upstream_v, one_hot_v, out_v, grad_v, sems
):
    made = copies(sems, (mask_ref, mask_v), (tokens_ref, tokens_v), (upstream_ref, upstream_v))
    tok = tokens_v.shape[0]
    live = tok // 2
    made[0].wait()
    mask = mask_v[...].astype(F32)
    before = lax.broadcasted_iota(jnp.int32, (tok, tok), 0) < lax.broadcasted_iota(jnp.int32, (tok, tok), 1)
    rank = dot(jnp.broadcast_to(mask, (8, tok)).astype(BF16), before.astype(F32).astype(BF16), 1, 0)[:1]
    column = lax.broadcasted_iota(jnp.int32, (1, tok), 1).astype(F32)
    place = jnp.where(mask > 0, rank, live + column - rank)
    row = lax.broadcasted_iota(jnp.int32, (tok, tok), 0).astype(F32)
    one_hot = (row == place).astype(F32).astype(BF16)
    one_hot_v[...] = one_hot
    made[1].wait()
    out_v[...] = dot(tokens_v[...], one_hot, 0, 1).astype(BF16)
    made[2].wait()
    out = copies(sems, (one_hot_v, one_hot_ref), (out_v, tokens_out))
    grad_v[...] = dot(upstream_v[...], one_hot[:live], 0, 1).astype(BF16)
    wait_all(out + copies(sems.at[pl.ds(2, 1)], (grad_v, grad_out)))


def order_tokens(tokens, upstream, loss_mask):
    tok, width = tokens.shape
    outs = [((tok, tok), BF16), ((width, tok), BF16), ((width, tok // 2), BF16)]
    return call(
        order_kernel,
        "order_tokens",
        (loss_mask.reshape(1, tok), tokens, upstream),
        outs,
        [
            pltpu.VMEM((1, tok), jnp.int32),
            pltpu.VMEM((tok, width), BF16),
            pltpu.VMEM((tok, width), BF16),
            *[pltpu.VMEM(*out) for out in outs],
            dma(3),
        ],
        3 * tok * tok * width,
        8 * tok * width,
        vmem=62 * 1024 * 1024,
    )


def row_columns(k, wide):
    row = (lax.axis_index("hid") // 4) ^ k
    return pl.ds(pl.multiple_of(row * wide, wide), wide)


def place(side, flipped):
    return (lax.axis_index("hid") % 4) ^ (2 * side + flipped)


def part_copies(total, rounded, outs, sems):
    width = total.shape[2] // 4
    keep_even, keep_odd, send_even, send_odd = outs
    pairs = []
    for i, (src, dst) in enumerate(((total, keep_even), (rounded, send_even), (rounded, keep_odd), (rounded, send_odd))):
        pairs.append((src.at[:, :, pl.ds(pl.multiple_of(place(i // 2, i % 2) * width, width), width)], dst))
    return copies(sems, *pairs)


def part_outs(rows, tok, width):
    return [((rows, tok, width), F32)] + 3 * [((rows, tok, width), BF16)]


def start_gate_up(gate_w, up_w, base, j, buffer, sem):
    wide = buffer.shape[1]
    for i, weight in enumerate((gate_w, up_w)):

        @pl.when(j % 2 == i)
        def _():
            pltpu.make_async_copy(weight.at[:, row_columns(base + j // 2, wide)], buffer, sem).start()


def start_down(down_w, j, buffer, sem):
    pltpu.make_async_copy(down_w.at[:, row_columns(j, buffer.shape[1])], buffer, sem).start()


def wait_block(down_w, buffer, sem):
    pltpu.make_async_copy(down_w.at[:, pl.ds(0, buffer.shape[1])], buffer, sem).wait()


def forward_kernel(
    mine, mine_last, other, other_last, gate_w, up_w, down_w, x_ref, hidden_t_ref, act_ref, slope_ref, *rest
):
    parts = rest[:4]
    x, w, acc, hidden_v, hidden_t_v, act_v, slope_v, total, rounded, sems, x_sems, w_sems, out_sems = rest[4:]
    slots = w.shape[0]
    rows = x.shape[0]
    steps = 2 * rows

    def start(j):
        slot = j % slots
        start_gate_up(gate_w, up_w, 0, j, w.at[slot], w_sems.at[slot])

    def start_last(j):
        start_down(down_w, j, w.at[j % slots], w_sems.at[j % slots])

    most = mine.shape[0]
    x_pairs = []
    for at, pieces in ((pl.ds(0, most), (mine, other)), (pl.ds(most, rows - most), (mine_last, other_last))):
        for side in range(2):
            for flipped, part in enumerate(pieces):
                x_pairs.append((part.at[:, side], x.at[at, place(side, flipped)]))
    x_in = copies(x_sems, *x_pairs)
    start(0)
    start(1)
    acc[...] = jnp.zeros_like(acc)

    def one(j):
        slot = j % slots

        @pl.when(j == 0)
        def _():
            wait_all(x_in[:4])

        @pl.when(j == 2 * most)
        def _():
            wait_all(x_in[4:])

        wait_block(gate_w, w.at[slot], w_sems.at[slot])

        @pl.when(j + 2 < steps)
        def _():
            start(j + 2)

        @pl.when(j + 2 >= steps)
        def _():
            start_last(j + 2 - steps)

        acc[j % 2] += dot(w[slot], x[j // 2].reshape(-1, x.shape[-1]), 1, 0)

    each(steps, one)
    live = act_v.shape[1]
    out = copies(sems, (x.at[:, :, :, pl.ds(0, live)], x_ref))
    gate_lin = acc[0]
    up_lin = acc[1]
    sig = jax.nn.sigmoid(gate_lin)
    act = gate_lin * sig
    hidden = (act * up_lin).astype(BF16)
    hidden_t_v[...] = hidden[:, :live]
    act_v[...] = act[:, :live]
    slope_v[...] = (up_lin * sig * (1.0 + gate_lin * (1.0 - sig)))[:, :live]
    hidden_v[...] = hidden.T
    out += copies(sems.at[pl.ds(1, 3)], (hidden_t_v, hidden_t_ref), (act_v, act_ref), (slope_v, slope_ref))

    def two(j):
        slot = j % slots
        wait_block(down_w, w.at[slot], w_sems.at[slot])

        @pl.when(j + 2 < rows)
        def _():
            start_last(j + 2)

        part = dot(hidden_v[...], w[slot], 1, 0)
        total[j] = part
        rounded[j] = part.astype(BF16)

    each(rows, two)
    wait_all(out + part_copies(total, rounded, parts, out_sems))


def forward(mine, other, gate_w, up_w, down_w, live):
    _, _, width, tok = mine[0].shape
    ff, features = gate_w.shape
    chips = features // (2 * width)
    rows, slots = chips // 2, 4
    return call(
        forward_kernel,
        "forward",
        (*mine, *other, gate_w, up_w, down_w),
        [
            ((rows, 4, width, live), BF16),
            ((ff, live), BF16),
            ((ff, live), F32),
            ((ff, live), F32),
            *part_outs(rows, tok, width),
        ],
        [
            pltpu.VMEM((rows, 4, width, tok), BF16),
            pltpu.VMEM((slots, ff, 4 * width), BF16),
            pltpu.VMEM((2, ff, tok), F32),
            pltpu.VMEM((tok, ff), BF16),
            pltpu.VMEM((ff, live), BF16),
            pltpu.VMEM((ff, live), F32),
            pltpu.VMEM((ff, live), F32),
            pltpu.VMEM((rows, tok, 4 * width), F32),
            pltpu.VMEM((rows, tok, 4 * width), BF16),
            dma(4),
            dma(2 * chips),
            dma(slots),
            dma(4 * rows),
        ],
        12 * chips * width * ff * tok,
        12 * chips * width * ff,
        vmem=48 * 1024 * 1024,
    )


def backward_kernel(
    mine, mine_odd, other, other_odd, act_ref, slope_ref, gate_w, up_w, down_w, g_ref, d_gate_ref, d_up_ref, *rest
):
    parts = rest[:4]
    g, act, slope, w, acc, *rest = rest[4:]
    d_hid, d_hid_t, total, rounded, sems, g_sems, w_sems, out_sems = rest
    slots = w.shape[0]
    rows = g.shape[0]
    steps = 2 * rows

    def start_first(j):
        start_down(down_w, j, w.at[j % slots], w_sems.at[j % slots])

    def start(j):
        slot = j % slots
        start_gate_up(gate_w, up_w, 0, j, w.at[slot], w_sems.at[slot])

    stacks = (mine, other, mine_odd, other_odd)
    first = copies(g_sems, *[(part, g.at[:, place(i // 2, i % 2)]) for i, part in enumerate(stacks)])
    start_first(0)
    start_first(1)
    late = copies(sems, (act_ref, act), (slope_ref, slope))
    acc[...] = jnp.zeros_like(acc)
    total[...] = jnp.zeros_like(total)
    wait_all(first)

    def one(j):
        slot = j % slots
        wait_block(down_w, w.at[slot], w_sems.at[slot])

        @pl.when(j + 2 < rows)
        def _():
            start_first(j + 2)

        @pl.when(j + 2 >= rows)
        def _():
            start(j + 2 - rows)

        acc[...] += dot(w[slot], g[j].reshape(-1, g.shape[-1]), 1, 0)

    each(rows, one)
    wait_all(late)
    d_gate = (acc[...] * slope[...]).astype(BF16)
    d_up = (acc[...] * act[...]).astype(BF16)
    d_hid_t[0] = d_gate
    d_hid_t[1] = d_up
    d_hid[0] = d_gate.T
    d_hid[1] = d_up.T
    out = copies(sems, (d_hid_t.at[0], d_gate_ref), (d_hid_t.at[1], d_up_ref), (g, g_ref))

    def two(j):
        slot = j % slots
        wait_block(gate_w, w.at[slot], w_sems.at[slot])

        @pl.when(j + 2 < steps)
        def _():
            start(j + 2)

        part = total[j // 2] + dot(d_hid[j % 2], w[slot], 1, 0)
        total[j // 2] = part
        rounded[j // 2] = part.astype(BF16)

    each(steps, two)
    wait_all(out + part_copies(total, rounded, parts, out_sems))


def backward(mine, other, act, slope, gate_w, up_w, down_w):
    _, width, live = mine[0].shape
    ff = act.shape[0]
    chips = down_w.shape[1] // (2 * width)
    rows, slots = chips // 2, 4
    d_hid_t = ((ff, live), BF16)
    return call(
        backward_kernel,
        "backward",
        (*mine, *other, act, slope, gate_w, up_w, down_w),
        [((rows, 4, width, live), BF16), d_hid_t, d_hid_t, *part_outs(rows, live, width)],
        [
            pltpu.VMEM((rows, 4, width, live), BF16),
            pltpu.VMEM((ff, live), F32),
            pltpu.VMEM((ff, live), F32),
            pltpu.VMEM((slots, ff, 4 * width), BF16),
            pltpu.VMEM((ff, live), F32),
            pltpu.VMEM((2, live, ff), BF16),
            pltpu.VMEM((2, ff, live), BF16),
            pltpu.VMEM((rows, live, 4 * width), F32),
            pltpu.VMEM((rows, live, 4 * width), BF16),
            dma(3),
            dma(2 * chips),
            dma(slots),
            dma(2 * chips),
        ],
        6 * live * down_w.size,
        6 * down_w.size,
        vmem=32 * 1024 * 1024,
    )


def weight_grad_kernel(hid_ref, x_ref, out_ref, hid, x, out_v, sems, out_sems):
    steps = out_v.shape[0]
    rows, wide, _ = x.shape
    half = wide // 2
    ready = copies(sems, (hid_ref, hid), (x_ref, x))

    def out_copy(j):
        row = (lax.axis_index("hid") // 4) ^ (j // 2)
        at = pl.ds(pl.multiple_of(row * wide + (j % 2) * half, half), half)
        return pltpu.make_async_copy(out_v.at[j], out_ref.at[:, at], out_sems.at[j])

    wait_all(ready)

    def step(j):
        out_v[j] = dot(hid[...], x[j // 2, pl.ds(pl.multiple_of((j % 2) * half, half), half), :], 1, 1).astype(BF16)
        out_copy(j).start()

    each(steps, step)
    wait_each(steps, out_copy)


def weight_grad(hid, x, name):
    rows, wide, live = x.shape
    ff = hid.shape[-2]
    steps = 2 * rows
    return call(
        weight_grad_kernel,
        name,
        (hid, x),
        [((ff, rows * wide), BF16)],
        [
            pltpu.VMEM((ff, live), BF16),
            pltpu.VMEM((rows, wide, live), BF16),
            pltpu.VMEM((steps, ff, wide // 2), BF16),
            dma(2),
            dma(steps),
        ],
        2 * live * ff * rows * wide,
        2 * ff * rows * wide,
        vmem=24 * 1024 * 1024,
    )[0]


def last_kernel(count, *refs):
    one_hot = refs[0][...]
    for i, out in enumerate(refs[-2:]):
        parts = refs[1 + i * count : 1 + (i + 1) * count]
        total = parts[0][...].astype(F32)
        for part in parts[1:]:
            total = total + part[...].astype(F32)
        out[...] = dot(one_hot[: total.shape[0]], total.astype(BF16), 0, 0).astype(BF16)


def last_sums(one_hot, first, second):
    tok = one_hot.shape[1]
    out = jax.ShapeDtypeStruct((tok, first[0].shape[1]), BF16)
    return pl.pallas_call(
        functools.partial(last_kernel, len(first)),
        out_shape=[out, out],
        compiler_params=params(),
        name="last_sums",
    )(one_hot, *first, *second)


def flip(x, bits):
    return lax.ppermute(x, "hid", [(i, i ^ bits) for i in range(16)])


def plus(a, b):
    return a.astype(F32) + b.astype(F32)


def join(*arrays):
    return lax.optimization_barrier(arrays)


def body16(tokens, upstream, loss_mask, gate_weight, up_weight, down_weight):
    tok, width = tokens.shape
    live = tok // 2
    gate_w, up_w = gate_weight.T, up_weight.T
    one_hot, x, g = order_tokens(tokens, upstream, loss_mask)
    z2, z1, y = flip(x, 8), flip(x, 4), flip(x, 2)
    yz1 = flip(z1, 2)
    yz1, y, z1, z2, g = join(yz1, y, z1, z2, g)
    z3, yz2, gz2 = flip(z2, 4), flip(z2, 2), flip(g, 8)
    gz2, yz2, z3, g = join(gz2, yz2, z3, g)
    yz3 = flip(z3, 2)
    most = jnp.stack([x, y, z1, yz1, z2, yz2]).reshape(3, 2, width, tok)
    most_other = flip(most, 1)
    gz3, gz1 = flip(g, 12), flip(g, 4)
    gz1, gz3, most_other, yz3 = join(gz1, gz3, most_other, yz3)
    g_even = jnp.stack([g, gz1, gz2, gz3])
    g_odd, g_even_other = flip(g_even, 2), flip(g_even, 1)
    last = jnp.stack([z3, yz3]).reshape(1, 2, width, tok)
    x_mine, x_other = (most, last), (most_other, flip(last, 1))
    x_rows, hidden_t, act, slope, keep_even, keep_odd, send_even, send_odd = forward(
        x_mine, x_other, gate_w, up_w, down_weight, live
    )
    send_odd, g_odd, g_even_other = join(send_odd, g_odd, g_even_other)
    recv_odd, g_odd_other = flip(send_odd, 1), flip(g_odd, 1)
    recv_odd, g_odd_other, send_even = join(recv_odd, g_odd_other, send_even)
    recv_even = flip(send_even, 1)
    out_y = flip(plus(keep_odd, recv_odd).astype(BF16), 2)
    g_rows, d_gate_t, d_up_t, t_keep_even, t_keep_odd, t_send_even, t_send_odd = backward(
        (g_even, g_odd), (g_even_other, g_odd_other), act, slope, gate_w, up_w, down_weight
    )
    t_send_odd, out_y, recv_even = join(t_send_odd, out_y, recv_even)
    t_recv_odd = flip(t_send_odd, 1)
    rows = [plus(keep_even[k], recv_even[k]) + out_y[k].astype(F32) for k in range(4)]
    z13 = flip(rows[3].astype(BF16), 4)
    t_recv_odd, t_send_even, hidden_t = join(t_recv_odd, t_send_even, hidden_t)
    t_recv_even = flip(t_send_even, 1)
    t_y23 = flip(plus(t_keep_odd[2:], t_recv_odd[2:]).astype(BF16), 2)
    down_grad = weight_grad(hidden_t, g_rows.reshape(4, 4 * width, live), "down_grad")
    down_grad, z13, t_y23, t_recv_odd, t_recv_even, d_gate_t = join(
        down_grad, z13, t_y23, t_recv_odd, t_recv_even, d_gate_t
    )
    t_even = plus(t_keep_even, t_recv_even)
    z2 = flip((rows[2] + z13.astype(F32)).astype(BF16), 8)
    z1 = flip(rows[1].astype(BF16), 4)
    t_y01 = flip(plus(t_keep_odd[:2], t_recv_odd[:2]).astype(BF16), 2)
    tz13 = flip((t_even[3] + t_y23[1].astype(F32)).astype(BF16), 4)
    x_rows = x_rows.reshape(4, 4 * width, live)
    gate_grad = weight_grad(d_gate_t, x_rows, "gate_grad")
    gate_grad, d_up_t, tz13, t_y01, z2, z1 = join(gate_grad, d_up_t, tz13, t_y01, z2, z1)
    tz1 = flip((t_even[1] + t_y01[1].astype(F32)).astype(BF16), 4)
    tz2 = flip((t_even[2] + plus(t_y23[0], tz13)).astype(BF16), 8)
    up_grad = weight_grad(d_up_t, x_rows, "up_grad")
    up_grad, tz2, tz1 = join(up_grad, tz2, tz1)
    t_row = t_even[0] + t_y01[0].astype(F32)
    ffn_output, token_grad = last_sums(one_hot, (rows[0], z2, z1), (t_row, tz2, tz1))
    return ffn_output, token_grad, gate_grad.T, up_grad.T, down_grad


def body_any(tokens, upstream, loss_mask, gate_weight, up_weight, down_weight):
    masked = upstream * loss_mask[:, None].astype(upstream.dtype)
    tokens = lax.all_gather(tokens, "hid", axis=1, tiled=True)
    grad = lax.all_gather(masked, "hid", axis=1, tiled=True)
    gate_lin = dot(tokens, gate_weight, 1, 0)
    up_lin = dot(tokens, up_weight, 1, 0)
    sig = jax.nn.sigmoid(gate_lin)
    act = gate_lin * sig
    hidden = (act * up_lin).astype(BF16)
    out = lax.psum_scatter(dot(down_weight, hidden, 0, 1), "hid", scatter_dimension=0, tiled=True)
    d_hidden = dot(grad, down_weight, 1, 1)
    d_up = (d_hidden * act).astype(BF16)
    d_gate = (d_hidden * up_lin * sig * (1.0 + gate_lin * (1.0 - sig))).astype(BF16)
    down_grad = dot(hidden, grad, 0, 0).astype(BF16)
    gate_grad = dot(tokens, d_gate, 0, 0).astype(BF16)
    up_grad = dot(tokens, d_up, 0, 0).astype(BF16)
    back = dot(gate_weight, d_gate, 1, 1) + dot(up_weight, d_up, 1, 1)
    back = lax.psum_scatter(back, "hid", scatter_dimension=0, tiled=True)
    return out.T.astype(BF16), back.T.astype(BF16), gate_grad, up_grad, down_grad


def solution(mesh):
    spec = P("groups", "hid")
    in_specs = (spec, spec, P("groups"), P(None, "hid"), P(None, "hid"), P("hid", None))
    out_specs = (spec, spec, spec, spec, P("hid", "groups"))
    body = body16 if mesh.shape["hid"] == 16 else body_any
    return jax.shard_map(body, mesh=mesh, in_specs=in_specs, out_specs=out_specs, check_vma=False)
```

```python
import functools

import jax
import jax.numpy as jnp
from jax import lax
from jax.experimental import pallas as pl
from jax.experimental.pallas import tpu as pltpu
from jax.sharding import PartitionSpec as P

F32 = jnp.float32
BF16 = jnp.bfloat16
VMEM_BYTES = 52 * 1024 * 1024


def dot(a, b, ca, cb):
    return lax.dot_general(a, b, (((ca,), (cb,)), ((), ())), preferred_element_type=F32)


def params():
    return pltpu.CompilerParams(vmem_limit_bytes=VMEM_BYTES)


def my_core():
    return lax.axis_index("hid") % 2


def chip_columns(k, width):
    chip = (lax.axis_index("hid") // 2) ^ k
    return pl.ds(pl.multiple_of(chip * (2 * width), 2 * width), 2 * width)


def call(kernel, name, operands, outs, scratch, flops, nbytes, vmem=VMEM_BYTES):
    return pl.pallas_call(
        kernel,
        in_specs=[pl.BlockSpec(memory_space=pl.ANY)] * len(operands),
        out_specs=[pl.BlockSpec(memory_space=pl.ANY)] * len(outs),
        out_shape=[jax.ShapeDtypeStruct(shape, kind) for shape, kind in outs],
        scratch_shapes=scratch,
        compiler_params=pltpu.CompilerParams(vmem_limit_bytes=vmem),
        cost_estimate=pl.CostEstimate(flops=flops, bytes_accessed=nbytes, transcendentals=0),
        name=name,
    )(*operands)


def copies(sems, *pairs):
    made = [pltpu.make_async_copy(src, dst, sems.at[i]) for i, (src, dst) in enumerate(pairs)]
    for c in made:
        c.start()
    return made


def wait_all(made):
    for c in made:
        c.wait()


def dma(count):
    return pltpu.SemaphoreType.DMA((count,))


def start_each(steps, make):
    def one(j, carry):
        make(j).start()
        return carry

    lax.fori_loop(0, steps, one, 0)


def wait_each(steps, make):
    def one(j, carry):
        make(j).wait()
        return carry

    lax.fori_loop(0, steps, one, 0)


def each(steps, body):
    def one(j, carry):
        body(j)
        return carry

    lax.fori_loop(0, steps, one, 0)


def stream(steps, ahead, make, body):
    for j in range(min(ahead, steps)):
        make(j).start()

    def one(j):
        make(j).wait()

        @pl.when(j + ahead < steps)
        def _():
            make(j + ahead).start()

        body(j)

    each(steps, one)


def order_kernel(
    mask_ref, tokens_ref, upstream_ref, one_hot_ref, tokens_out, grad_out, mask_v, tokens_v, upstream_v, one_hot_v, out_v, grad_v, sems
):
    made = copies(sems, (mask_ref, mask_v), (tokens_ref, tokens_v), (upstream_ref, upstream_v))
    tok = tokens_v.shape[0]
    live = tok // 2
    made[0].wait()
    mask = mask_v[...].astype(F32)
    before = lax.broadcasted_iota(jnp.int32, (tok, tok), 0) < lax.broadcasted_iota(jnp.int32, (tok, tok), 1)
    rank = dot(jnp.broadcast_to(mask, (8, tok)).astype(BF16), before.astype(F32).astype(BF16), 1, 0)[:1]
    column = lax.broadcasted_iota(jnp.int32, (1, tok), 1).astype(F32)
    place = jnp.where(mask > 0, rank, live + column - rank)
    row = lax.broadcasted_iota(jnp.int32, (tok, tok), 0).astype(F32)
    one_hot = (row == place).astype(F32).astype(BF16)
    one_hot_v[...] = one_hot
    made[1].wait()
    out_v[...] = dot(tokens_v[...], one_hot, 0, 1).astype(BF16)
    made[2].wait()
    out = copies(sems, (one_hot_v, one_hot_ref), (out_v, tokens_out))
    grad_v[...] = dot(upstream_v[...], one_hot[:live], 0, 1).astype(BF16)
    wait_all(out + copies(sems.at[pl.ds(2, 1)], (grad_v, grad_out)))


def order_tokens(tokens, upstream, loss_mask):
    tok, width = tokens.shape
    outs = [((tok, tok), BF16), ((width, tok), BF16), ((width, tok // 2), BF16)]
    return call(
        order_kernel,
        "order_tokens",
        (loss_mask.reshape(1, tok), tokens, upstream),
        outs,
        [
            pltpu.VMEM((1, tok), jnp.int32),
            pltpu.VMEM((tok, width), BF16),
            pltpu.VMEM((tok, width), BF16),
            *[pltpu.VMEM(*out) for out in outs],
            dma(3),
        ],
        3 * tok * tok * width,
        8 * tok * width,
        vmem=62 * 1024 * 1024,
    )


def row_columns(k, wide):
    row = (lax.axis_index("hid") // 4) ^ k
    return pl.ds(pl.multiple_of(row * wide, wide), wide)


def place(side, flipped):
    return (lax.axis_index("hid") % 4) ^ (2 * side + flipped)


def part_copies(total, rounded, outs, sems):
    width = total.shape[2] // 4
    keep_even, keep_odd, send_even, send_odd = outs
    pairs = []
    for i, (src, dst) in enumerate(((total, keep_even), (rounded, send_even), (rounded, keep_odd), (rounded, send_odd))):
        pairs.append((src.at[:, :, pl.ds(pl.multiple_of(place(i // 2, i % 2) * width, width), width)], dst))
    return copies(sems, *pairs)


def part_outs(rows, tok, width):
    return [((rows, tok, width), F32)] + 3 * [((rows, tok, width), BF16)]


def start_gate_up(gate_w, up_w, base, j, buffer, sem):
    wide = buffer.shape[1]
    for i, weight in enumerate((gate_w, up_w)):

        @pl.when(j % 2 == i)
        def _():
            pltpu.make_async_copy(weight.at[:, row_columns(base + j // 2, wide)], buffer, sem).start()


def start_down(down_w, j, buffer, sem):
    pltpu.make_async_copy(down_w.at[:, row_columns(j, buffer.shape[1])], buffer, sem).start()


def wait_block(down_w, buffer, sem):
    pltpu.make_async_copy(down_w.at[:, pl.ds(0, buffer.shape[1])], buffer, sem).wait()


def forward_kernel(
    mine, mine_last, other, other_last, gate_w, up_w, down_w, x_ref, hidden_t_ref, act_ref, slope_ref, *rest
):
    parts = rest[:4]
    x, w, acc, hidden_v, hidden_t_v, act_v, slope_v, total, rounded, sems, x_sems, w_sems, out_sems = rest[4:]
    slots = w.shape[0]
    rows = x.shape[0]
    steps = 2 * rows

    def start(j):
        slot = j % slots
        start_gate_up(gate_w, up_w, 0, j, w.at[slot], w_sems.at[slot])

    def start_last(j):
        start_down(down_w, j, w.at[j % slots], w_sems.at[j % slots])

    most = mine.shape[0]
    x_pairs = []
    for at, pieces in ((pl.ds(0, most), (mine, other)), (pl.ds(most, rows - most), (mine_last, other_last))):
        for side in range(2):
            for flipped, part in enumerate(pieces):
                x_pairs.append((part.at[:, side], x.at[at, place(side, flipped)]))
    x_in = copies(x_sems, *x_pairs)
    start(0)
    start(1)
    acc[...] = jnp.zeros_like(acc)

    def one(j):
        slot = j % slots

        @pl.when(j == 0)
        def _():
            wait_all(x_in[:4])

        @pl.when(j == 2 * most)
        def _():
            wait_all(x_in[4:])

        wait_block(gate_w, w.at[slot], w_sems.at[slot])

        @pl.when(j + 2 < steps)
        def _():
            start(j + 2)

        @pl.when(j + 2 >= steps)
        def _():
            start_last(j + 2 - steps)

        acc[j % 2] += dot(w[slot], x[j // 2].reshape(-1, x.shape[-1]), 1, 0)

    each(steps, one)
    live = act_v.shape[1]
    out = copies(sems, (x.at[:, :, :, pl.ds(0, live)], x_ref))
    gate_lin = acc[0]
    up_lin = acc[1]
    sig = jax.nn.sigmoid(gate_lin)
    act = gate_lin * sig
    hidden = (act * up_lin).astype(BF16)
    hidden_t_v[...] = hidden[:, :live]
    act_v[...] = act[:, :live]
    slope_v[...] = (up_lin * sig * (1.0 + gate_lin * (1.0 - sig)))[:, :live]
    hidden_v[...] = hidden.T
    out += copies(sems.at[pl.ds(1, 3)], (hidden_t_v, hidden_t_ref), (act_v, act_ref), (slope_v, slope_ref))

    def two(j):
        slot = j % slots
        wait_block(down_w, w.at[slot], w_sems.at[slot])

        @pl.when(j + 2 < rows)
        def _():
            start_last(j + 2)

        part = dot(hidden_v[...], w[slot], 1, 0)
        total[j] = part
        rounded[j] = part.astype(BF16)

    each(rows, two)
    wait_all(out + part_copies(total, rounded, parts, out_sems))


def forward(mine, other, gate_w, up_w, down_w, live):
    _, _, width, tok = mine[0].shape
    ff, features = gate_w.shape
    chips = features // (2 * width)
    rows, slots = chips // 2, 4
    return call(
        forward_kernel,
        "forward",
        (*mine, *other, gate_w, up_w, down_w),
        [
            ((rows, 4, width, live), BF16),
            ((ff, live), BF16),
            ((ff, live), F32),
            ((ff, live), F32),
            *part_outs(rows, tok, width),
        ],
        [
            pltpu.VMEM((rows, 4, width, tok), BF16),
            pltpu.VMEM((slots, ff, 4 * width), BF16),
            pltpu.VMEM((2, ff, tok), F32),
            pltpu.VMEM((tok, ff), BF16),
            pltpu.VMEM((ff, live), BF16),
            pltpu.VMEM((ff, live), F32),
            pltpu.VMEM((ff, live), F32),
            pltpu.VMEM((rows, tok, 4 * width), F32),
            pltpu.VMEM((rows, tok, 4 * width), BF16),
            dma(4),
            dma(2 * chips),
            dma(slots),
            dma(4 * rows),
        ],
        12 * chips * width * ff * tok,
        12 * chips * width * ff,
        vmem=48 * 1024 * 1024,
    )


def backward_kernel(
    mine, mine_odd, other, other_odd, act_ref, slope_ref, gate_w, up_w, down_w, g_ref, d_gate_ref, d_up_ref, *rest
):
    parts = rest[:4]
    g, act, slope, w, acc, *rest = rest[4:]
    d_hid, d_hid_t, total, rounded, sems, g_sems, w_sems, out_sems = rest
    slots = w.shape[0]
    rows = g.shape[0]
    steps = 2 * rows

    def start_first(j):
        start_down(down_w, j, w.at[j % slots], w_sems.at[j % slots])

    def start(j):
        slot = j % slots
        start_gate_up(gate_w, up_w, 0, j, w.at[slot], w_sems.at[slot])

    stacks = (mine, other, mine_odd, other_odd)
    first = copies(g_sems, *[(part, g.at[:, place(i // 2, i % 2)]) for i, part in enumerate(stacks)])
    start_first(0)
    start_first(1)
    late = copies(sems, (act_ref, act), (slope_ref, slope))
    acc[...] = jnp.zeros_like(acc)
    total[...] = jnp.zeros_like(total)
    wait_all(first)

    def one(j):
        slot = j % slots
        wait_block(down_w, w.at[slot], w_sems.at[slot])

        @pl.when(j + 2 < rows)
        def _():
            start_first(j + 2)

        @pl.when(j + 2 >= rows)
        def _():
            start(j + 2 - rows)

        acc[...] += dot(w[slot], g[j].reshape(-1, g.shape[-1]), 1, 0)

    each(rows, one)
    wait_all(late)
    d_gate = (acc[...] * slope[...]).astype(BF16)
    d_up = (acc[...] * act[...]).astype(BF16)
    d_hid_t[0] = d_gate
    d_hid_t[1] = d_up
    d_hid[0] = d_gate.T
    d_hid[1] = d_up.T
    out = copies(sems, (d_hid_t.at[0], d_gate_ref), (d_hid_t.at[1], d_up_ref), (g, g_ref))

    def two(j):
        slot = j % slots
        wait_block(gate_w, w.at[slot], w_sems.at[slot])

        @pl.when(j + 2 < steps)
        def _():
            start(j + 2)

        part = total[j // 2] + dot(d_hid[j % 2], w[slot], 1, 0)
        total[j // 2] = part
        rounded[j // 2] = part.astype(BF16)

    each(steps, two)
    wait_all(out + part_copies(total, rounded, parts, out_sems))


def backward(mine, other, act, slope, gate_w, up_w, down_w):
    _, width, live = mine[0].shape
    ff = act.shape[0]
    chips = down_w.shape[1] // (2 * width)
    rows, slots = chips // 2, 4
    d_hid_t = ((ff, live), BF16)
    return call(
        backward_kernel,
        "backward",
        (*mine, *other, act, slope, gate_w, up_w, down_w),
        [((rows, 4, width, live), BF16), d_hid_t, d_hid_t, *part_outs(rows, live, width)],
        [
            pltpu.VMEM((rows, 4, width, live), BF16),
            pltpu.VMEM((ff, live), F32),
            pltpu.VMEM((ff, live), F32),
            pltpu.VMEM((slots, ff, 4 * width), BF16),
            pltpu.VMEM((ff, live), F32),
            pltpu.VMEM((2, live, ff), BF16),
            pltpu.VMEM((2, ff, live), BF16),
            pltpu.VMEM((rows, live, 4 * width), F32),
            pltpu.VMEM((rows, live, 4 * width), BF16),
            dma(3),
            dma(2 * chips),
            dma(slots),
            dma(2 * chips),
        ],
        6 * live * down_w.size,
        6 * down_w.size,
        vmem=32 * 1024 * 1024,
    )


def weight_grad_kernel(hid_ref, x_ref, out_ref, hid, x, out_v, sems, out_sems):
    steps = out_v.shape[0]
    rows, wide, _ = x.shape
    half = wide // 2
    ready = copies(sems, (hid_ref, hid), (x_ref, x))

    def out_copy(j):
        row = (lax.axis_index("hid") // 4) ^ (j // 2)
        at = pl.ds(pl.multiple_of(row * wide + (j % 2) * half, half), half)
        return pltpu.make_async_copy(out_v.at[j], out_ref.at[:, at], out_sems.at[j])

    wait_all(ready)

    def step(j):
        out_v[j] = dot(hid[...], x[j // 2, pl.ds(pl.multiple_of((j % 2) * half, half), half), :], 1, 1).astype(BF16)
        out_copy(j).start()

    each(steps, step)
    wait_each(steps, out_copy)


def weight_grad(hid, x, name):
    rows, wide, live = x.shape
    ff = hid.shape[-2]
    steps = 2 * rows
    return call(
        weight_grad_kernel,
        name,
        (hid, x),
        [((ff, rows * wide), BF16)],
        [
            pltpu.VMEM((ff, live), BF16),
            pltpu.VMEM((rows, wide, live), BF16),
            pltpu.VMEM((steps, ff, wide // 2), BF16),
            dma(2),
            dma(steps),
        ],
        2 * live * ff * rows * wide,
        2 * ff * rows * wide,
        vmem=24 * 1024 * 1024,
    )[0]


def last_kernel(count, *refs):
    one_hot = refs[0][...]
    for i, out in enumerate(refs[-2:]):
        parts = refs[1 + i * count : 1 + (i + 1) * count]
        total = parts[0][...].astype(F32)
        for part in parts[1:]:
            total = total + part[...].astype(F32)
        out[...] = dot(one_hot[: total.shape[0]], total.astype(BF16), 0, 0).astype(BF16)


def last_sums(one_hot, first, second):
    tok = one_hot.shape[1]
    out = jax.ShapeDtypeStruct((tok, first[0].shape[1]), BF16)
    return pl.pallas_call(
        functools.partial(last_kernel, len(first)),
        out_shape=[out, out],
        compiler_params=params(),
        name="last_sums",
    )(one_hot, *first, *second)


def flip(x, bits):
    return lax.ppermute(x, "hid", [(i, i ^ bits) for i in range(16)])


def plus(a, b):
    return a.astype(F32) + b.astype(F32)


def join(*arrays):
    return lax.optimization_barrier(arrays)


def body16(tokens, upstream, loss_mask, gate_weight, up_weight, down_weight):
    tok, width = tokens.shape
    live = tok // 2
    gate_w, up_w = gate_weight.T, up_weight.T
    one_hot, x, g = order_tokens(tokens, upstream, loss_mask)
    z2, z1, y = flip(x, 8), flip(x, 4), flip(x, 2)
    z1, g = join(z1, g)
    yz1 = flip(z1, 2)
    y, z2, g = join(y, z2, g)
    z3, yz2, gz2, gz1 = flip(z2, 4), flip(z2, 2), flip(g, 8), flip(g, 4)
    gz1, gz2, yz1, yz2, z3, g = join(gz1, gz2, yz1, yz2, z3, g)
    yz3 = flip(z3, 2)
    most = jnp.stack([x, y, z1, yz1, z2, yz2]).reshape(3, 2, width, tok)
    most_other = flip(most, 1)
    gz3 = flip(g, 12)
    gz3, most_other, yz3 = join(gz3, most_other, yz3)
    g_even = jnp.stack([g, gz1, gz2, gz3])
    g_odd, g_even_other = flip(g_even, 2), flip(g_even, 1)
    last = jnp.stack([z3, yz3]).reshape(1, 2, width, tok)
    x_mine, x_other = (most, last), (most_other, flip(last, 1))
    x_rows, hidden_t, act, slope, keep_even, keep_odd, send_even, send_odd = forward(
        x_mine, x_other, gate_w, up_w, down_weight, live
    )
    send_odd, g_odd, g_even_other = join(send_odd, g_odd, g_even_other)
    recv_odd, g_odd_other = flip(send_odd, 1), flip(g_odd, 1)
    recv_odd, g_odd_other, send_even = join(recv_odd, g_odd_other, send_even)
    recv_even = flip(send_even, 1)
    out_y = flip(plus(keep_odd, recv_odd).astype(BF16), 2)
    g_rows, d_gate_t, d_up_t, t_keep_even, t_keep_odd, t_send_even, t_send_odd = backward(
        (g_even, g_odd), (g_even_other, g_odd_other), act, slope, gate_w, up_w, down_weight
    )
    t_send_odd, out_y, recv_even = join(t_send_odd, out_y, recv_even)
    t_recv_odd = flip(t_send_odd, 1)
    rows = [plus(keep_even[k], recv_even[k]) + out_y[k].astype(F32) for k in range(4)]
    z13 = flip(rows[3].astype(BF16), 4)
    t_recv_odd, t_send_even, hidden_t = join(t_recv_odd, t_send_even, hidden_t)
    t_recv_even = flip(t_send_even, 1)
    t_y23 = flip(plus(t_keep_odd[2:], t_recv_odd[2:]).astype(BF16), 2)
    down_grad = weight_grad(hidden_t, g_rows.reshape(4, 4 * width, live), "down_grad")
    down_grad, z13, t_y23, t_recv_odd, t_recv_even, d_gate_t = join(
        down_grad, z13, t_y23, t_recv_odd, t_recv_even, d_gate_t
    )
    t_even = plus(t_keep_even, t_recv_even)
    z2 = flip((rows[2] + z13.astype(F32)).astype(BF16), 8)
    z1 = flip(rows[1].astype(BF16), 4)
    t_y01 = flip(plus(t_keep_odd[:2], t_recv_odd[:2]).astype(BF16), 2)
    tz13 = flip((t_even[3] + t_y23[1].astype(F32)).astype(BF16), 4)
    x_rows = x_rows.reshape(4, 4 * width, live)
    gate_grad = weight_grad(d_gate_t, x_rows, "gate_grad")
    gate_grad, d_up_t, tz13, t_y01, z2, z1 = join(gate_grad, d_up_t, tz13, t_y01, z2, z1)
    tz1 = flip((t_even[1] + t_y01[1].astype(F32)).astype(BF16), 4)
    tz2 = flip((t_even[2] + plus(t_y23[0], tz13)).astype(BF16), 8)
    up_grad = weight_grad(d_up_t, x_rows, "up_grad")
    up_grad, tz2, tz1 = join(up_grad, tz2, tz1)
    t_row = t_even[0] + t_y01[0].astype(F32)
    ffn_output, token_grad = last_sums(one_hot, (rows[0], z2, z1), (t_row, tz2, tz1))
    return ffn_output, token_grad, gate_grad.T, up_grad.T, down_grad


def body_any(tokens, upstream, loss_mask, gate_weight, up_weight, down_weight):
    masked = upstream * loss_mask[:, None].astype(upstream.dtype)
    tokens = lax.all_gather(tokens, "hid", axis=1, tiled=True)
    grad = lax.all_gather(masked, "hid", axis=1, tiled=True)
    gate_lin = dot(tokens, gate_weight, 1, 0)
    up_lin = dot(tokens, up_weight, 1, 0)
    sig = jax.nn.sigmoid(gate_lin)
    act = gate_lin * sig
    hidden = (act * up_lin).astype(BF16)
    out = lax.psum_scatter(dot(down_weight, hidden, 0, 1), "hid", scatter_dimension=0, tiled=True)
    d_hidden = dot(grad, down_weight, 1, 1)
    d_up = (d_hidden * act).astype(BF16)
    d_gate = (d_hidden * up_lin * sig * (1.0 + gate_lin * (1.0 - sig))).astype(BF16)
    down_grad = dot(hidden, grad, 0, 0).astype(BF16)
    gate_grad = dot(tokens, d_gate, 0, 0).astype(BF16)
    up_grad = dot(tokens, d_up, 0, 0).astype(BF16)
    back = dot(gate_weight, d_gate, 1, 1) + dot(up_weight, d_up, 1, 1)
    back = lax.psum_scatter(back, "hid", scatter_dimension=0, tiled=True)
    return out.T.astype(BF16), back.T.astype(BF16), gate_grad, up_grad, down_grad


def solution(mesh):
    spec = P("groups", "hid")
    in_specs = (spec, spec, P("groups"), P(None, "hid"), P(None, "hid"), P("hid", None))
    out_specs = (spec, spec, spec, spec, P("hid", "groups"))
    body = body16 if mesh.shape["hid"] == 16 else body_any
    return jax.shard_map(body, mesh=mesh, in_specs=in_specs, out_specs=out_specs, check_vma=False)
```
